1024 devices in a mesh: px: 64 (over y, x, core), py: 16 (over z).
Axes of the slice: x: 4, y: 8, z: 16, core: 2. Of those that a mesh axis runs over, the one named last changes fastest.
Arguments:
- velocity: float32 [2, 20, 128, 2048], P(None, None, 'px', 'py'), may hold values from -6 to 6
- direction: float32 [2, 20, 128, 2048], P(None, None, 'px', 'py'), may hold values from -2 to 2
- forcing: float32 [2, 20, 128, 2048], P(None, None, 'px', 'py'), may hold values from -6 to 6
- softness: float32 [128, 2048], P('px', 'py'), may hold values from 0.5 to 2
- friction: float32 [128, 2048], P('px', 'py'), may hold values from 0.3 to 3
- links: int32 [4, 128, 2048], P(None, 'px', 'py'), may hold values from 0 to 8
- aggregate: int32 [128, 2048], P('px', 'py'), may hold values from 0 to 63
- coarse_diag: float32 [65536], P('px'), may hold values from 1 to 3
- coarse_vals: float32 [4, 65536], P(None, 'px'), may hold values from -0.2 to 0.2
- coarse_cols: int32 [4, 65536], P(None, 'px'), may hold values from 0 to 1023
Outputs:
- image: float32 [2, 20, 128, 2048], P(None, None, 'px', 'py')
- answer: float32 [2, 20, 128, 2048], P(None, None, 'px', 'py')
The draws below stay inside these ranges and needn't reach their ends.
Inputs may be any that keep to these rules, and one draw needn't show every extreme that they name: `links`: 0 to 7 name one of the eight surrounding columns in the order of the steps, 8 an unused slot; a column may name a direction twice. `aggregate`: ids are local to a device. `coarse_cols`: numbers count the aggregates of one subgroup.
All inputs are finite; a program needn't handle non-finite values.
Results may differ from the reference program's by a relative error of at most 0.00029.
Values sent between devices are 32-bit elements; how exact they have to be, the bound alone decides.
A program may use at most 32 MiB of HBM per device.

```python
import math
import jax
import jax.numpy as jnp
from jax import lax

CX = 2
CY = 128
LAYERS = 20
SLOTS = 4
COARSE_LINKS = 4
CITERS = 4
AGG_DEV = 64
NX = 128
NY = 2048
COARSE = 65536
N_PX = 64
N_PY = 16


def plant(entries, key, low, largest):
    dims = entries.shape
    index_at = [jax.random.randint(jax.random.fold_in(key, axis), (), 0, dims[axis]) for axis in range(len(dims))]
    entries = entries.at[tuple(index_at)].set(low)
    longest = dims.index(max(dims))
    index_at[longest] = (index_at[longest] + 1) % dims[longest]
    return entries.at[tuple(index_at)].set(largest)


def steps_of(stream_key, dims, cuts, low, largest):
    def one(dim, blocks):
        draws = jax.random.uniform(jax.random.fold_in(jax.random.fold_in(stream_key, 6), dim), (blocks,), jnp.float32, low / len(cuts), largest / len(cuts))
        return jnp.repeat(jnp.exp(draws), dims[dim] // blocks).reshape((-1,) + (1,) * (len(dims) - dim - 1))

    gain = one(*cuts[0])
    for cut in cuts[1:]:
        gain = gain * one(*cut)
    return gain


def bell_draw(own_key, dims, scale, reach, shards=(), held_as=jnp.bfloat16):
    factor_of = steps_of(own_key, dims, shards, -0.22, 0.18) if shards else 1.0
    values = jax.random.normal(own_key, dims, jnp.float32) * scale * factor_of
    return jnp.minimum(jnp.maximum(values, -reach), reach).astype(held_as)


def setup_inputs(seed: int = 0) -> dict:
    arg_keys = jax.random.split(jax.random.key(seed), 11)
    velocity = bell_draw(arg_keys[0], (2, LAYERS, NX, NY), 1.0, 6.0, ((2, 64), (3, 16)), jnp.float32)
    direction = bell_draw(arg_keys[1], (2, LAYERS, NX, NY), 0.3, 2.0, ((2, 64), (3, 16)), jnp.float32)
    forcing = bell_draw(arg_keys[2], (2, LAYERS, NX, NY), 1.0, 6.0, ((2, 64), (3, 16)), jnp.float32)
    softness = jnp.clip(jnp.exp(math.log(2.0) - 1.3862944 * jax.random.uniform(arg_keys[3], (NX, NY), jnp.float32) ** steps_of(arg_keys[3], (NX, NY), ((0, 64), (1, 16)), -0.2, 0.2)), 0.5, 2.0)
    friction = jnp.clip(jnp.exp(math.log(3.0) - 2.3025851 * jax.random.uniform(arg_keys[4], (NX, NY), jnp.float32) ** steps_of(arg_keys[4], (NX, NY), ((0, 64), (1, 16)), -0.2, 0.2)), 0.3, 3.0)
    links = plant(jax.random.randint(arg_keys[5], (SLOTS, NX, NY), 0, 9), jax.random.fold_in(arg_keys[5], 1), 0, 8).astype(jnp.int32)
    aggregate = plant(jax.random.randint(arg_keys[6], (NX, NY), 0, AGG_DEV), jax.random.fold_in(arg_keys[6], 1), 0, AGG_DEV - 1).astype(jnp.int32)
    coarse_diag = jnp.clip(jnp.exp(math.log(3.0) - 1.0986123 * jax.random.uniform(arg_keys[7], (COARSE,), jnp.float32) ** steps_of(arg_keys[7], (COARSE,), ((0, 64),), -0.2, 0.2)), 1.0, 3.0)
    coarse_vals = jnp.clip(jax.random.uniform(arg_keys[8], (COARSE_LINKS, COARSE), jnp.float32, -0.2, 0.2) * steps_of(arg_keys[8], (COARSE_LINKS, COARSE), ((1, 64),), -0.4, 0.0), -0.2, 0.2)
    coarse_cols = plant(jax.random.randint(arg_keys[9], (COARSE_LINKS, COARSE), 0, AGG_DEV * N_PY), jax.random.fold_in(arg_keys[9], 1), 0, (AGG_DEV * N_PY) - 1).astype(jnp.int32)
    return {"velocity": velocity, "direction": direction, "forcing": forcing, "softness": softness, "friction": friction, "links": links, "aggregate": aggregate, "coarse_diag": coarse_diag, "coarse_vals": coarse_vals, "coarse_cols": coarse_cols}


KZ = 4.0
EPS0 = 0.05
OMEGA = 0.8
OFFSETS = ((-1, -1), (-1, 0), (-1, 1), (0, -1), (0, 1), (1, -1), (1, 0), (1, 1))


def link_counts(links):
    codes = jnp.arange(8, dtype=jnp.int32)
    return jnp.sum((links[None] == codes[:, None, None, None]).astype(jnp.float32), axis=1)


def viscosity(field, rate):
    above = jnp.concatenate([field[:, 1:], field[:, -1:]], axis=1)
    below = jnp.concatenate([field[:, :1], field[:, :-1]], axis=1)
    shear = above - below
    strain = EPS0 + 0.25 * KZ * jnp.sum(shear * shear, axis=0)
    return rate * jnp.power(strain, -1.0 / 3.0)


def neighbours(extended, shift_x, shift_y):
    height = extended.shape[-2] - 2
    width = extended.shape[-1] - 2
    return extended[..., 1 + shift_x:1 + shift_x + height, 1 + shift_y:1 + shift_y + width]


def operator(field_ext, rate_ext, friction, counts):
    eta_ext = viscosity(field_ext, rate_ext)
    field = neighbours(field_ext, 0, 0)
    eta = neighbours(eta_ext, 0, 0)
    face = 0.5 * (eta[:-1] + eta[1:])
    flux = KZ * face * (field[:, 1:] - field[:, :-1])
    empty = jnp.zeros_like(flux[:, :1])
    result = jnp.concatenate([empty, flux], axis=1) - jnp.concatenate([flux, empty], axis=1)
    result = result + jnp.concatenate([friction * field[:, :1], jnp.zeros_like(field[:, 1:])], axis=1)
    for number, (shift_x, shift_y) in enumerate(OFFSETS):
        coupling = counts[number] * 0.5 * (eta + neighbours(eta_ext, shift_x, shift_y))
        result = result + coupling * (field - neighbours(field_ext, shift_x, shift_y))
    return result


def line_factors(eta_ext, friction, counts):
    eta = neighbours(eta_ext, 0, 0)
    depth = eta.shape[0]
    face = 0.5 * (eta[:-1] + eta[1:])
    side = jnp.zeros_like(eta)
    for number, (shift_x, shift_y) in enumerate(OFFSETS):
        side = side + counts[number] * 0.5 * (eta + neighbours(eta_ext, shift_x, shift_y))
    lowers, pivots, ratios = [], [], []
    for level in range(depth):
        middle = side[level]
        if level > 0:
            middle = middle + KZ * face[level - 1]
        if level < depth - 1:
            middle = middle + KZ * face[level]
        if level == 0:
            middle = middle + friction
            lowers.append(jnp.zeros_like(middle))
            pivot = middle
        else:
            lower = -KZ * face[level - 1]
            lowers.append(lower)
            pivot = middle - lower * ratios[level - 1]
        pivots.append(pivot)
        if level < depth - 1:
            ratios.append(-KZ * face[level] / pivot)
        else:
            ratios.append(jnp.zeros_like(pivot))
    return lowers, pivots, ratios


def line_solve(factors, rhs):
    lowers, pivots, ratios = factors
    depth = len(pivots)
    forward = [rhs[:, 0] / pivots[0]]
    for level in range(1, depth):
        forward.append((rhs[:, level] - lowers[level] * forward[level - 1]) / pivots[level])
    backward = [None] * depth
    backward[depth - 1] = forward[depth - 1]
    for level in range(depth - 2, -1, -1):
        backward[level] = forward[level] - ratios[level] * backward[level + 1]
    return jnp.stack(backward, axis=1)


def jacobi_sweep(mine, whole, target, diag, vals, cols):
    applied = diag * mine
    for slot in range(vals.shape[0]):
        applied = applied + vals[slot] * whole[:, cols[slot]]
    return mine + OMEGA * (target - applied) / diag


def pad_field(field):
    return jnp.pad(field, ((0, 0), (0, 0), (1, 1), (1, 1)))


def join_blocks(parts):
    return jnp.moveaxis(parts, 0, 2).reshape(2, LAYERS, NX, NY)


def reference(velocity, direction, forcing, softness, friction, links, aggregate, coarse_diag, coarse_vals, coarse_cols):
    state_pad = pad_field(velocity)
    probe_pad = pad_field(direction)
    rate_pad = jnp.pad(softness, 1)
    counts = link_counts(links)
    blocks = jnp.arange(N_PX, dtype=jnp.int32)

    def rows_of(array, index, width, axis):
        return lax.dynamic_slice_in_dim(array, index * CX, width, axis)

    def local_parts(index):
        state_ext = rows_of(state_pad, index, CX + 2, 2)
        rate_ext = rows_of(rate_pad, index, CX + 2, 0)
        rub = rows_of(friction, index, CX, 0)
        tally = rows_of(counts, index, CX, 1)

        def apply_op(field_ext):
            return operator(field_ext, rate_ext, rub, tally)

        def jacobian(step_ext):
            return jax.jvp(apply_op, (state_ext,), (step_ext,))[1]

        factors = line_factors(viscosity(state_ext, rate_ext), rub, tally)
        return jacobian, factors

    def first_section(index):
        jacobian, factors = local_parts(index)
        image = jacobian(rows_of(probe_pad, index, CX + 2, 2))
        resid = rows_of(forcing, index, CX, 2) - image
        return image, line_solve(factors, resid)

    image_parts, smooth_parts = lax.map(first_section, blocks)
    image = join_blocks(image_parts)
    smooth = join_blocks(smooth_parts)
    resid = forcing - image
    smooth_pad = pad_field(smooth)

    def second_section(index):
        jacobian, factors = local_parts(index)
        after = rows_of(resid, index, CX, 2) - jacobian(rows_of(smooth_pad, index, CX + 2, 2))
        return jnp.sum(after, axis=1) / LAYERS

    column_mean = jnp.moveaxis(lax.map(second_section, blocks), 0, 1).reshape(2, NX, NY)
    group = AGG_DEV * N_PY
    row_ids = jnp.arange(NX, dtype=jnp.int32) // CX
    col_ids = jnp.arange(NY, dtype=jnp.int32) // CY
    segment = row_ids[:, None] * group + col_ids[None, :] * AGG_DEV + aggregate
    restricted = jax.ops.segment_sum(column_mean.reshape(2, -1).T, segment.reshape(-1), num_segments=COARSE).T
    offset = (jnp.arange(COARSE, dtype=jnp.int32) // group) * group
    global_cols = coarse_cols + offset[None, :]
    iterate = jnp.zeros((2, COARSE), jnp.float32)
    for sweep in range(CITERS):
        iterate = jacobi_sweep(iterate, iterate, restricted, coarse_diag, coarse_vals, global_cols)
    correction = iterate[:, segment]
    coarse_step = smooth + correction[:, None]
    coarse_pad = pad_field(coarse_step)

    def third_section(index):
        jacobian, factors = local_parts(index)
        final = rows_of(resid, index, CX, 2) - jacobian(rows_of(coarse_pad, index, CX + 2, 2))
        return rows_of(coarse_step, index, CX, 2) + line_solve(factors, final)

    answer = join_blocks(lax.map(third_section, blocks))
    return image, answer
```

```python
import functools

import jax
import jax.numpy as jnp
from jax import lax
from jax.experimental import pallas as pl
from jax.experimental.pallas import tpu as pltpu
from jax.sharding import PartitionSpec as P

CITERS = 4
AGG_DEV = 64
KZ = 4.0
EPS0 = 0.05
OMEGA = 0.8
OFFSETS = ((-1, -1), (-1, 0), (-1, 1), (0, -1), (0, 1), (1, -1), (1, 0), (1, 1))
MESH = pl.DeviceIdType.MESH
LAYERS = 20
F32 = jnp.float32
I32 = jnp.int32

FIELD = 64


def turn(x, shift, axis):
    shift %= x.shape[axis]
    return pltpu.roll(x, shift, axis) if shift else x


def stacked(tiles):
    return jnp.concatenate([t[None] for t in tiles], axis=0)


def vertical(x):
    return jnp.concatenate([x[1:], x[-1:]], axis=0) - jnp.concatenate([x[:1], x[:-1]], axis=0)


def kernel(
    n_px,
    n_py,
    velocity,
    direction,
    forcing,
    softness,
    friction,
    links,
    aggregate,
    coarse_diag,
    coarse_vals,
    coarse_cols,
    image_out,
    answer_out,
    vx,
    vx_recv,
    fo,
    fr,
    lk,
    ag,
    dg,
    cv,
    cc,
    edge_send,
    edge_recv,
    sm,
    sm_recv,
    edge2_send,
    edge2_recv,
    rs,
    rr,
    xs,
    ct,
    cr,
    cs,
    ds_,
    ws,
    img,
    ans,
    load_sem,
    send_sem,
    recv_sem,
    out_sem,
):
    px = lax.axis_index("px")
    py = lax.axis_index("py")
    n_hi = n_py // 2

    def wrap(value, count):
        return lax.rem(value + count, count)

    def peer(dx, dy):
        return (wrap(px + dx, n_px), wrap(py + dy, n_py))

    loads = []

    def load(src, dst):
        copy = pltpu.make_async_copy(src, dst, load_sem.at[len(loads)])
        copy.start()
        loads.append(copy)

    for c in range(2):
        own = pl.ds(4 * c + 1, 2)
        load(velocity.at[c], vx.at[pl.ds(0, LAYERS), own])
        load(direction.at[c], vx.at[pl.ds(LAYERS, LAYERS), own])
        load(softness, vx.at[2 * LAYERS, own])
        load(aggregate, ag.at[own])
    first_loads = len(loads)

    sides = [(dx, dy) for dx in (-1, 0, 1) for dy in (-1, 0, 1) if (dx, dy) != (0, 0)]
    peers = [peer(dx, dy) for dx, dy in sides if dx != 0] + [peer(0, k) for k in range(1, n_py)]
    barrier = pltpu.get_barrier_semaphore()
    for target in peers:
        pl.semaphore_signal(barrier, inc=1, device_id=target, device_id_type=MESH)

    for c in range(2):
        own = pl.ds(4 * c + 1, 2)
        load(forcing.at[c], fo.at[:, own])
        load(friction, fr.at[own])
        load(links, lk.at[:, own])
    load(coarse_diag, dg)
    for k in range(4):
        load(coarse_vals.at[:, k], cv.at[k])
        load(coarse_cols.at[:, k], cc.at[k])

    lane = lax.broadcasted_iota(I32, (8, 128), 1)
    sub = lax.broadcasted_iota(I32, (8, 128), 0)
    row = sub & 3
    core = (row == 1) | (row == 2)
    none = 9
    row_ok = (row != jnp.where(px > 0, none, 0)) & (row != jnp.where(px < n_px - 1, none, 3))
    even = (lane & 1) == 0
    no_left = jnp.where(py > 0, none, 0)
    no_right = jnp.where(py < n_py - 1, none, 1)
    edge_ok = row_ok & ((lane & 1) != no_left) & ((lane & 1) != no_right)

    def packed(fields):
        tile = jnp.zeros((8, 128), F32)
        for x, at in fields:
            tile = jnp.where((lane >> 1) == at // 2, turn(x, at + 1, 1), tile)
        return tile

    count = [0]

    def send(src, dst, target):
        i = count[0]
        count[0] += 1
        copy = pltpu.make_async_remote_copy(
            src_ref=src,
            dst_ref=dst,
            send_sem=send_sem.at[i],
            recv_sem=recv_sem.at[i],
            device_id=target,
            device_id_type=MESH,
        )
        copy.start()
        return copy

    def exchange_rim(src, dst, tile, tiles):
        copies = []
        for i, (dx, dy) in enumerate((dx, dy) for dy in (-1, 1) for dx in (-1, 0, 1)):
            copies.append(send(tile, tiles.at[5 - i], peer(dx, dy)))
        for c in range(2):
            copies.append(
                send(src.at[:, pl.ds(4 * c + 2, 1)], dst.at[:, pl.ds(4 * c, 1)], peer(1, 0))
            )
            copies.append(
                send(src.at[:, pl.ds(4 * c + 1, 1)], dst.at[:, pl.ds(4 * c + 3, 1)], peer(-1, 0))
            )
        return copies

    def edges_of(tiles):
        def column(first):
            below, here, above = tiles[first], tiles[first + 1], tiles[first + 2]
            return jnp.where(
                row == 0, turn(below, -2, 0), jnp.where(row == 3, turn(above, 2, 0), here)
            )

        left, right = column(0), column(3)
        return jnp.where(edge_ok, jnp.where(even, left, turn(right, -2, 1)), 0.0)

    def unpacked(tile, at):
        return stacked([turn(tile, -(at + 2 * layer), 1) for layer in range(LAYERS)])

    def beside(x, ends):
        left = jnp.where(lane == 0, ends, turn(x, 1, x.ndim - 1))
        right = jnp.where(lane == 127, ends, turn(x, -1, x.ndim - 1))
        return left, x, right

    for copy in loads[:first_loads]:
        copy.wait()
    agg_own = jnp.where(core, ag[...], 0)
    edge_send[...] = packed(
        [(vx[layer], 2 * layer) for layer in range(LAYERS)]
        + [(vx[2 * LAYERS], 2 * LAYERS), (agg_own.astype(F32), 2 * LAYERS + 2)]
        + [(vx[LAYERS + layer], FIELD + 2 * layer) for layer in range(LAYERS)]
    )
    pl.semaphore_wait(barrier, len(peers))
    round1 = exchange_rim(vx, vx_recv, edge_send, edge_recv)

    for copy in loads[first_loads:]:
        copy.wait()
    rub = jnp.where(core, fr[...], 1.0)
    slots = jnp.where(core, lk[...], 8)
    halves = []
    for d, (dx, _) in enumerate(OFFSETS):
        tally = jnp.sum((slots == d).astype(F32), axis=0)
        halves.append(turn(0.5 * tally, dx, 0))
    scale = OMEGA / dg[...]
    weights = [cv[k] * scale for k in range(4)]
    cols = [cc[k] for k in range(4)]
    col_hi = [c >> 7 for c in cols]
    col_lo = [c & 127 for c in cols]

    for copy in round1:
        copy.wait_recv()

    def joined(own, rim):
        return jnp.where(row_ok, jnp.where(core, own, rim), 0.0)

    v = joined(vx[0:LAYERS], vx_recv[0:LAYERS])
    rate = joined(vx[2 * LAYERS], vx_recv[2 * LAYERS])
    edge = edges_of(edge_recv)
    top = (lane == 38) | (lane == 37) | (lane == 102) | (lane == 101)
    bottom = (lane == 0) | (lane == 127) | (lane == 64) | (lane == 63)

    def edge_vertical(tile):
        return jnp.where(top, tile, turn(tile, -2, 1)) - jnp.where(bottom, tile, turn(tile, 2, 1))

    def viscosity(shear, soft, axis):
        square = shear * shear
        strain = EPS0 + 0.25 * KZ * (square + turn(square, 4, axis))
        eta = soft * jnp.exp(jnp.log(strain) * (-1.0 / 3.0))
        slope = (-2.0 / 3.0 * 0.25 * KZ) * eta / strain * shear
        return eta, slope

    eta, slope = viscosity(vertical(v), rate, 1)
    edge_shear = edge_vertical(edge)
    edge_rate = jnp.where(even, edge[:, 40:41], edge[:, 39:40])
    edge_eta, edge_slope = viscosity(edge_shear, edge_rate, 0)
    edge_slope = turn(edge_slope, FIELD, 1)
    v_beside = beside(v, unpacked(edge, 0))
    eta_beside = beside(eta, unpacked(edge_eta, 0))

    side = jnp.zeros_like(v)
    pull = jnp.zeros_like(v)
    for dx in (-1, 0, 1):
        eta_here = turn(eta, dx, 1)
        v_here = turn(v, dx, 1)
        side_part = jnp.zeros_like(v)
        pull_part = jnp.zeros_like(v)
        for d, (ox, oy) in enumerate(OFFSETS):
            if ox != dx:
                continue
            couple = halves[d] * (eta_here + eta_beside[oy + 1])
            drop = halves[d] * (v_here - v_beside[oy + 1])
            cs[d] = couple
            ds_[d] = drop
            side_part = side_part + couple
            pull_part = pull_part + drop
        side = side + turn(side_part, -dx, 1)
        pull = pull + turn(pull_part, -dx, 1)
    face = (0.5 * KZ) * (eta[:-1] + eta[1:])
    jump = (0.5 * KZ) * (v[1:] - v[:-1])

    def jacobian(x, x_edge):
        rise = slope * vertical(x)
        deta = rise + turn(rise, 4, 1)
        edge_rise = edge_slope * edge_vertical(x_edge)
        edge_deta = edge_rise + turn(edge_rise, 4, 0)
        x_beside = beside(x, unpacked(x_edge, FIELD))
        deta_beside = beside(deta, unpacked(edge_deta, FIELD))
        total = side * x + pull * deta
        for dx in (-1, 0, 1):
            part = jnp.zeros_like(x)
            for d, (ox, oy) in enumerate(OFFSETS):
                if ox != dx:
                    continue
                part = part + (ds_[d] * deta_beside[oy + 1] - cs[d] * x_beside[oy + 1])
            total = total + turn(part, -dx, 1)
        flux = face * (x[1:] - x[:-1]) + jump * (deta[1:] + deta[:-1])
        empty = jnp.zeros_like(flux[:1])
        total = total + jnp.concatenate([rub * x[:1] - flux[:1], flux[:-1] - flux[1:], flux[-1:]])
        return total

    x = joined(vx[LAYERS : 2 * LAYERS], vx_recv[LAYERS : 2 * LAYERS])
    image = jacobian(x, edge)
    img[...] = image
    outs = []
    for c in range(2):
        copy = pltpu.make_async_copy(
            img.at[:, pl.ds(4 * c + 1, 2)], image_out.at[c], out_sem.at[c]
        )
        copy.start()
        outs.append(copy)
    resid = jnp.where(core, fo[...], 0.0) - image

    inverse, lower, upper = [], [], []
    for layer in range(LAYERS):
        pivot = side[layer]
        if layer == 0:
            pivot = pivot + rub + face[0]
        else:
            pivot = pivot + face[layer - 1] - face[layer - 1] * upper[layer - 1]
            if layer < LAYERS - 1:
                pivot = pivot + face[layer]
        inv = 1.0 / pivot
        inverse.append(inv)
        lower.append(face[layer - 1] * inv if layer else None)
        upper.append(face[layer] * inv if layer < LAYERS - 1 else None)

    def line_solve(rhs):
        forward = [rhs[0] * inverse[0]]
        for layer in range(1, LAYERS):
            forward.append(rhs[layer] * inverse[layer] + lower[layer] * forward[-1])
        back = [forward[-1]]
        for layer in range(LAYERS - 2, -1, -1):
            back.append(forward[layer] + upper[layer] * back[-1])
        return back[::-1]

    smooth = stacked(line_solve([resid[layer] for layer in range(LAYERS)]))
    sm[...] = smooth
    edge2_send[...] = packed([(smooth[layer], FIELD + 2 * layer) for layer in range(LAYERS)])

    round2 = exchange_rim(sm, sm_recv, edge2_send, edge2_recv)
    agg_rows = [agg_own[r : r + 1, :] for r in (1, 2)]
    ids = lax.broadcasted_iota(I32, (128, 128), 0) & (AGG_DEV - 1)
    hot = [(ids == a).astype(F32) for a in agg_rows]
    for copy in round2:
        copy.wait_recv()
    smooth_ext = joined(sm[...], sm_recv[...])
    after = resid - jacobian(smooth_ext, edges_of(edge2_recv))
    mean = jnp.where(core, jnp.sum(after, axis=0) / LAYERS, 0.0)

    sums = [
        lax.dot_general(
            mean, h, (((1,), (1,)), ((), ())),
            precision=lax.Precision.HIGHEST, preferred_element_type=F32,
        )
        for h in hot
    ]
    first = sums[0][1:2] + sums[1][2:3]
    second = sums[0][5:6] + sums[1][6:7]
    mine = jnp.where(lane[0:1] < AGG_DEV, first, second)
    rs[0] = mine
    place = lax.rem(py, 2) * n_hi + lax.div(py, 2)
    round3 = []
    for k in range(1, n_py):
        round3.append(send(rs, rr.at[pl.ds(place, 1)], peer(0, k)))
    rr[place] = mine

    for d, (dx, _) in enumerate(OFFSETS):
        ws[:, d] = turn(cs[d], -dx, 1)
    rest = line_solve([after[layer] for layer in range(LAYERS)])
    for layer in range(LAYERS):
        ans[layer] = smooth[layer] + rest[layer]
    held = ws[0] * inverse[0]
    ws[0] = held
    for layer in range(1, LAYERS):
        held = ws[layer] * inverse[layer] + lower[layer] * held
        ws[layer] = held
    for layer in range(LAYERS - 2, -1, -1):
        held = ws[layer] + upper[layer] * held
        ws[layer] = held

    for copy in round3:
        copy.wait_recv()
    evens, odds = rr[0:n_hi, 0, :], rr[n_hi : 2 * n_hi, 0, :]
    low = lax.broadcasted_iota(I32, (n_hi, 128), 1) < AGG_DEV
    target = [
        jnp.where(low, evens, turn(odds, AGG_DEV, 1)) * scale,
        jnp.where(low, turn(evens, AGG_DEV, 1), odds) * scale,
    ]

    def picked(source, at):
        return jnp.take_along_axis(source, at, axis=1, mode="promise_in_bounds")

    iterate = target
    for _ in range(CITERS - 1):
        later = []
        for c in range(2):
            rows = [
                jnp.broadcast_to(iterate[c][h : h + 1], (n_hi, 128)) for h in range(n_hi)
            ]
            value = (1.0 - OMEGA) * iterate[c] + target[c]
            for k in range(4):
                found = picked(rows[0], col_lo[k])
                for h in range(1, n_hi):
                    found = jnp.where(col_hi[k] == h, picked(rows[h], col_lo[k]), found)
                value = value - weights[k] * found
            later.append(value)
        iterate = later
    xs[0] = iterate[0]
    xs[1] = iterate[1]

    def corrected(owner, at):
        h = lax.div(owner, 2)
        source = jnp.where(
            sub < 4,
            jnp.broadcast_to(xs[0, pl.ds(h, 1), :], (8, 128)),
            jnp.broadcast_to(xs[1, pl.ds(h, 1), :], (8, 128)),
        )
        return picked(source, at + AGG_DEV * lax.rem(owner, 2))

    edge_agg = edge.astype(I32)
    agg_left = jnp.broadcast_to(edge_agg[:, 42:43], (8, 128))
    agg_right = jnp.broadcast_to(edge_agg[:, 41:42], (8, 128))
    corr = corrected(py, agg_own)
    corr_edge = jnp.where(
        lane < 64,
        corrected(wrap(py - 1, n_py), agg_left),
        corrected(wrap(py + 1, n_py), agg_right),
    )
    half = lane >> 6
    corr_edge = jnp.where((half != no_left) & (half != no_right), corr_edge, 0.0)
    ct[0] = corr
    ct[1] = corr_edge

    round4 = [send(ct, cr.at[0], peer(1, 0)), send(ct, cr.at[1], peer(-1, 0))]
    for copy in round4:
        copy.wait_recv()

    def rows_joined(i, own):
        joined = jnp.where(
            row == 0, turn(cr[0, i], -2, 0), jnp.where(row == 3, turn(cr[1, i], 2, 0), own)
        )
        return jnp.where(row_ok, joined, 0.0)

    corr_beside = beside(rows_joined(0, corr), rows_joined(1, corr_edge))
    result = ans[...]
    for d, (dx, dy) in enumerate(OFFSETS):
        result = result + ws[:, d] * turn(corr_beside[dy + 1], -dx, 0)
    ans[...] = result
    for c in range(2):
        copy = pltpu.make_async_copy(
            ans.at[:, pl.ds(4 * c + 1, 2)], answer_out.at[c], out_sem.at[2 + c]
        )
        copy.start()
        outs.append(copy)
    for copy in round1 + round2 + round3 + round4:
        copy.wait_send()
    for copy in outs:
        copy.wait()


def solution(mesh):
    n_px, n_py = mesh.shape["px"], mesh.shape["py"]
    n_hi = n_py // 2
    n_sends = 10 + 10 + (n_py - 1) + 2

    def body(
        velocity, direction, forcing, softness, friction, links, aggregate, diag, vals, cols
    ):
        block = jax.ShapeDtypeStruct(velocity.shape, F32)
        return pl.pallas_call(
            functools.partial(kernel, n_px, n_py),
            out_shape=(block, block),
            in_specs=[pl.BlockSpec(memory_space=pltpu.HBM)] * 10,
            out_specs=[pl.BlockSpec(memory_space=pltpu.HBM)] * 2,
            scratch_shapes=[
                pltpu.VMEM((2 * LAYERS + 1, 8, 128), F32),
                pltpu.VMEM((2 * LAYERS + 1, 8, 128), F32),
                pltpu.VMEM((LAYERS, 8, 128), F32),
                pltpu.VMEM((8, 128), F32),
                pltpu.VMEM((4, 8, 128), I32),
                pltpu.VMEM((8, 128), I32),
                pltpu.VMEM((n_hi, 128), F32),
                pltpu.VMEM((4, n_hi, 128), F32),
                pltpu.VMEM((4, n_hi, 128), I32),
                pltpu.VMEM((8, 128), F32),
                pltpu.VMEM((6, 8, 128), F32),
                pltpu.VMEM((LAYERS, 8, 128), F32),
                pltpu.VMEM((LAYERS, 8, 128), F32),
                pltpu.VMEM((8, 128), F32),
                pltpu.VMEM((6, 8, 128), F32),
                pltpu.VMEM((1, 1, 128), F32),
                pltpu.VMEM((n_py, 1, 128), F32),
                pltpu.VMEM((2, n_hi, 128), F32),
                pltpu.VMEM((2, 8, 128), F32),
                pltpu.VMEM((2, 2, 8, 128), F32),
                pltpu.VMEM((8, LAYERS, 8, 128), F32),
                pltpu.VMEM((8, LAYERS, 8, 128), F32),
                pltpu.VMEM((LAYERS, 8, 8, 128), F32),
                pltpu.VMEM((LAYERS, 8, 128), F32),
                pltpu.VMEM((LAYERS, 8, 128), F32),
                pltpu.SemaphoreType.DMA((23,)),
                pltpu.SemaphoreType.DMA((n_sends,)),
                pltpu.SemaphoreType.DMA((n_sends,)),
                pltpu.SemaphoreType.DMA((4,)),
            ],
            compiler_params=pltpu.CompilerParams(
                collective_id=0, has_side_effects=True, vmem_limit_bytes=32 * 1024 * 1024
            ),
        )(
            velocity,
            direction,
            forcing,
            softness,
            friction,
            links,
            aggregate,
            diag.reshape(n_hi, 128),
            vals.reshape(4, n_hi, 128).transpose(1, 0, 2),
            cols.reshape(4, n_hi, 128).transpose(1, 0, 2),
        )

    return jax.shard_map(
        body,
        mesh=mesh,
        in_specs=(
            P(None, None, "px", "py"),
            P(None, None, "px", "py"),
            P(None, None, "px", "py"),
            P("px", "py"),
            P("px", "py"),
            P(None, "px", "py"),
            P("px", "py"),
            P("px"),
            P(None, "px"),
            P(None, "px"),
        ),
        out_specs=(P(None, None, "px", "py"), P(None, None, "px", "py")),
        check_vma=False,
    )
```

```python
import functools

import jax
import jax.numpy as jnp
from jax import lax
from jax.experimental import pallas as pl
from jax.experimental.pallas import tpu as pltpu
from jax.sharding import PartitionSpec as P

CITERS = 4
AGG_DEV = 64
KZ = 4.0
EPS0 = 0.05
OMEGA = 0.8
OFFSETS = ((-1, -1), (-1, 0), (-1, 1), (0, -1), (0, 1), (1, -1), (1, 0), (1, 1))
MESH = pl.DeviceIdType.MESH
LAYERS = 20
F32 = jnp.float32
I32 = jnp.int32

FIELD = 64
REACH = 3


def turn(x, shift, axis):
    shift %= x.shape[axis]
    return pltpu.roll(x, shift, axis) if shift else x


def stacked(tiles):
    return jnp.concatenate([t[None] for t in tiles], axis=0)


def vertical(x):
    return jnp.concatenate([x[1:], x[-1:]], axis=0) - jnp.concatenate([x[:1], x[:-1]], axis=0)


def kernel(
    n_px,
    n_py,
    velocity,
    direction,
    forcing,
    softness,
    friction,
    links,
    aggregate,
    coarse_diag,
    coarse_vals,
    coarse_cols,
    img,
    ans,
    vx,
    vx_recv,
    fo,
    fr,
    lk,
    ag,
    dg,
    cv,
    cc,
    edge_send,
    edge_recv,
    sm,
    sm_recv,
    edge2_send,
    edge2_recv,
    rs,
    rr,
    xs,
    ct,
    cr,
    cs,
    ds_,
    ws,
    load_sem,
    send_sem,
    recv_sem,
    relay,
):
    px = lax.axis_index("px")
    py = lax.axis_index("py")
    n_hi = n_py // 2

    def wrap(value, count):
        return lax.rem(value + count, count)

    def peer(dx, dy):
        return (wrap(px + dx, n_px), wrap(py + dy, n_py))

    sides = [(dx, dy) for dx in (-1, 1) for dy in (-1, 1, 0)]
    near = [k for k in range(1, n_py) if min(k, n_py - k) <= REACH]
    peers = [peer(dx, dy) for dx, dy in sides] + [peer(0, k) for k in near]
    barrier = pltpu.get_barrier_semaphore()
    for target in peers:
        pl.semaphore_signal(barrier, inc=1, device_id=target, device_id_type=MESH)
    stages = -(-(n_py // 2) // REACH) - 1

    def relay_signal(stage):
        if stage < stages:
            for k in (REACH, n_py - REACH):
                pl.semaphore_signal(
                    relay.at[stage], inc=1, device_id=peer(0, k), device_id_type=MESH
                )

    def relay_wait(stage):
        if stage < stages:
            pl.semaphore_wait(relay.at[stage], 2)

    loads = []

    def load(src, dst):
        copy = pltpu.make_async_copy(src, dst, load_sem.at[len(loads)])
        copy.start()
        loads.append(copy)

    for c in range(2):
        own = pl.ds(4 * c + 1, 2)
        load(velocity.at[c], vx.at[pl.ds(0, LAYERS), own])
        load(direction.at[c], vx.at[pl.ds(LAYERS, LAYERS), own])
        load(softness, vx.at[2 * LAYERS, own])
        load(aggregate, ag.at[own])
    first_loads = len(loads)

    for c in range(2):
        own = pl.ds(4 * c + 1, 2)
        load(forcing.at[c], fo.at[:, own])
        load(friction, fr.at[own])
        load(links, lk.at[:, own])
    load(coarse_diag, dg)
    for k in range(4):
        load(coarse_vals.at[:, k], cv.at[k])
        load(coarse_cols.at[:, k], cc.at[k])

    lane = lax.broadcasted_iota(I32, (8, 128), 1)
    sub = lax.broadcasted_iota(I32, (8, 128), 0)
    row = sub & 3
    core = (row == 1) | (row == 2)
    none = 9
    row_ok = (row != jnp.where(px > 0, none, 0)) & (row != jnp.where(px < n_px - 1, none, 3))
    even = (lane & 1) == 0
    no_left = jnp.where(py > 0, none, 0)
    no_right = jnp.where(py < n_py - 1, none, 1)
    edge_ok = row_ok & ((lane & 1) != no_left) & ((lane & 1) != no_right)

    def packed(fields):
        tile = jnp.zeros((8, 128), F32)
        for x, at in fields:
            tile = jnp.where((lane >> 1) == at // 2, turn(x, at + 1, 1), tile)
        return tile

    count = [0]

    def send(src, dst, target):
        i = count[0]
        count[0] += 1
        copy = pltpu.make_async_remote_copy(
            src_ref=src,
            dst_ref=dst,
            send_sem=send_sem.at[i],
            recv_sem=recv_sem.at[i],
            device_id=target,
            device_id_type=MESH,
        )
        copy.start()
        return copy

    def exchange_rim(src, dst, tile, tiles):
        slot = {(dx, dy): 3 * (dy > 0) + dx + 1 for dx in (-1, 0, 1) for dy in (-1, 1)}
        copies = []

        def tile_to(dx, dy):
            copies.append(send(tile, tiles.at[slot[-dx, -dy]], peer(dx, dy)))

        for dx in (-1, 1):
            for dy in (-1, 1):
                tile_to(dx, dy)
        for c in range(2):
            copies.append(
                send(src.at[:, pl.ds(4 * c + 2, 1)], dst.at[:, pl.ds(4 * c, 1)], peer(1, 0))
            )
            copies.append(
                send(src.at[:, pl.ds(4 * c + 1, 1)], dst.at[:, pl.ds(4 * c + 3, 1)], peer(-1, 0))
            )
        for dy in (-1, 1):
            tile_to(0, dy)
        return copies

    def edges_of(tiles):
        def column(first):
            below, here, above = tiles[first], tiles[first + 1], tiles[first + 2]
            return jnp.where(
                row == 0, turn(below, -2, 0), jnp.where(row == 3, turn(above, 2, 0), here)
            )

        left, right = column(0), column(3)
        return jnp.where(edge_ok, jnp.where(even, left, turn(right, -2, 1)), 0.0)

    def unpacked(tile, at):
        return stacked([turn(tile, -(at + 2 * layer), 1) for layer in range(LAYERS)])

    def beside(x, ends):
        left = jnp.where(lane == 0, ends, turn(x, 1, x.ndim - 1))
        right = jnp.where(lane == 127, ends, turn(x, -1, x.ndim - 1))
        return left, x, right

    for copy in loads[:first_loads]:
        copy.wait()
    agg_own = jnp.where(core, ag[...], 0)
    edge_send[...] = packed(
        [(vx[layer], 2 * layer) for layer in range(LAYERS)]
        + [(vx[2 * LAYERS], 2 * LAYERS), (agg_own.astype(F32), 2 * LAYERS + 2)]
        + [(vx[LAYERS + layer], FIELD + 2 * layer) for layer in range(LAYERS)]
    )
    pl.semaphore_wait(barrier, len(peers))
    relay_signal(0)
    round1 = exchange_rim(vx, vx_recv, edge_send, edge_recv)

    for copy in loads[first_loads:]:
        copy.wait()
    rub = jnp.where(core, fr[...], 1.0)
    slots = jnp.where(core, lk[...], 8)
    halves = []
    for d, (dx, _) in enumerate(OFFSETS):
        tally = jnp.sum((slots == d).astype(F32), axis=0)
        halves.append(turn(0.5 * tally, dx, 0))
    scale = OMEGA / dg[...]
    weights = [cv[k] * scale for k in range(4)]
    cols = [cc[k] for k in range(4)]
    col_hi = [c >> 7 for c in cols]
    col_lo = [c & 127 for c in cols]

    for copy in round1:
        copy.wait_recv()

    relay_wait(0)
    relay_signal(1)

    def joined(own, rim):
        return jnp.where(row_ok, jnp.where(core, own, rim), 0.0)

    v = joined(vx[0:LAYERS], vx_recv[0:LAYERS])
    rate = joined(vx[2 * LAYERS], vx_recv[2 * LAYERS])
    edge = edges_of(edge_recv)
    top = (lane == 38) | (lane == 37) | (lane == 102) | (lane == 101)
    bottom = (lane == 0) | (lane == 127) | (lane == 64) | (lane == 63)

    def edge_vertical(tile):
        return jnp.where(top, tile, turn(tile, -2, 1)) - jnp.where(bottom, tile, turn(tile, 2, 1))

    def viscosity(shear, soft, axis):
        square = shear * shear
        strain = EPS0 + 0.25 * KZ * (square + turn(square, 4, axis))
        eta = soft * jnp.exp(jnp.log(strain) * (-1.0 / 3.0))
        slope = (-2.0 / 3.0 * 0.25 * KZ) * eta / strain * shear
        return eta, slope

    eta, slope = viscosity(vertical(v), rate, 1)
    edge_shear = edge_vertical(edge)
    edge_rate = jnp.where(even, edge[:, 40:41], edge[:, 39:40])
    edge_eta, edge_slope = viscosity(edge_shear, edge_rate, 0)
    edge_slope = turn(edge_slope, FIELD, 1)
    v_beside = beside(v, unpacked(edge, 0))
    eta_beside = beside(eta, unpacked(edge_eta, 0))

    side = jnp.zeros_like(v)
    pull = jnp.zeros_like(v)
    for dx in (-1, 0, 1):
        eta_here = turn(eta, dx, 1)
        v_here = turn(v, dx, 1)
        side_part = jnp.zeros_like(v)
        pull_part = jnp.zeros_like(v)
        for d, (ox, oy) in enumerate(OFFSETS):
            if ox != dx:
                continue
            couple = halves[d] * (eta_here + eta_beside[oy + 1])
            drop = halves[d] * (v_here - v_beside[oy + 1])
            cs[d] = couple
            ds_[d] = drop
            side_part = side_part + couple
            pull_part = pull_part + drop
        side = side + turn(side_part, -dx, 1)
        pull = pull + turn(pull_part, -dx, 1)
    face = (0.5 * KZ) * (eta[:-1] + eta[1:])
    jump = (0.5 * KZ) * (v[1:] - v[:-1])

    def jacobian(x, x_edge):
        rise = slope * vertical(x)
        deta = rise + turn(rise, 4, 1)
        edge_rise = edge_slope * edge_vertical(x_edge)
        edge_deta = edge_rise + turn(edge_rise, 4, 0)
        x_beside = beside(x, unpacked(x_edge, FIELD))
        deta_beside = beside(deta, unpacked(edge_deta, FIELD))
        total = side * x + pull * deta
        for dx in (-1, 0, 1):
            part = jnp.zeros_like(x)
            for d, (ox, oy) in enumerate(OFFSETS):
                if ox != dx:
                    continue
                part = part + (ds_[d] * deta_beside[oy + 1] - cs[d] * x_beside[oy + 1])
            total = total + turn(part, -dx, 1)
        flux = face * (x[1:] - x[:-1]) + jump * (deta[1:] + deta[:-1])
        empty = jnp.zeros_like(flux[:1])
        total = total + jnp.concatenate([rub * x[:1] - flux[:1], flux[:-1] - flux[1:], flux[-1:]])
        return total

    x = joined(vx[LAYERS : 2 * LAYERS], vx_recv[LAYERS : 2 * LAYERS])
    image = jacobian(x, edge)
    img[...] = image
    resid = jnp.where(core, fo[...], 0.0) - image

    inverse, lower, upper = [], [], []
    for layer in range(LAYERS):
        pivot = side[layer]
        if layer == 0:
            pivot = pivot + rub + face[0]
        else:
            pivot = pivot + face[layer - 1] - face[layer - 1] * upper[layer - 1]
            if layer < LAYERS - 1:
                pivot = pivot + face[layer]
        inv = 1.0 / pivot
        inverse.append(inv)
        lower.append(face[layer - 1] * inv if layer else None)
        upper.append(face[layer] * inv if layer < LAYERS - 1 else None)

    def line_solve(rhs):
        forward = [rhs[0] * inverse[0]]
        for layer in range(1, LAYERS):
            forward.append(rhs[layer] * inverse[layer] + lower[layer] * forward[-1])
        back = [forward[-1]]
        for layer in range(LAYERS - 2, -1, -1):
            back.append(forward[layer] + upper[layer] * back[-1])
        return back[::-1]

    smooth = stacked(line_solve([resid[layer] for layer in range(LAYERS)]))
    sm[...] = smooth
    edge2_send[...] = packed([(smooth[layer], FIELD + 2 * layer) for layer in range(LAYERS)])

    round2 = exchange_rim(sm, sm_recv, edge2_send, edge2_recv)
    agg_rows = [agg_own[r : r + 1, :] for r in (1, 2)]
    ids = lax.broadcasted_iota(I32, (128, 128), 0) & (AGG_DEV - 1)
    hot = [(ids == a).astype(F32) for a in agg_rows]
    for copy in round2:
        copy.wait_recv()
    relay_wait(1)
    smooth_ext = joined(sm[...], sm_recv[...])
    after = resid - jacobian(smooth_ext, edges_of(edge2_recv))
    mean = jnp.where(core, jnp.sum(after, axis=0) / LAYERS, 0.0)

    sums = [
        lax.dot_general(
            mean, h, (((1,), (1,)), ((), ())),
            precision=lax.Precision.HIGHEST, preferred_element_type=F32,
        )
        for h in hot
    ]
    first = sums[0][1:2] + sums[1][2:3]
    second = sums[0][5:6] + sums[1][6:7]
    mine = jnp.where(lane[0:1] < AGG_DEV, first, second)
    rs[0] = mine
    place = lax.rem(py, 2) * n_hi + lax.div(py, 2)
    round3 = []
    for k in sorted(range(1, n_py), key=lambda k: -min(k, n_py - k)):
        round3.append(send(rs, rr.at[pl.ds(place, 1)], peer(0, k)))
    rr[place] = mine

    for d, (dx, _) in enumerate(OFFSETS):
        ws[:, d] = turn(cs[d], -dx, 1)
    rest = line_solve([after[layer] for layer in range(LAYERS)])
    for layer in range(LAYERS):
        ans[layer] = smooth[layer] + rest[layer]
    held = ws[0] * inverse[0]
    ws[0] = held
    for layer in range(1, LAYERS):
        held = ws[layer] * inverse[layer] + lower[layer] * held
        ws[layer] = held
    for layer in range(LAYERS - 2, -1, -1):
        held = ws[layer] + upper[layer] * held
        ws[layer] = held

    for copy in round3:
        copy.wait_recv()
    evens, odds = rr[0:n_hi, 0, :], rr[n_hi : 2 * n_hi, 0, :]
    low = lax.broadcasted_iota(I32, (n_hi, 128), 1) < AGG_DEV
    target = [
        jnp.where(low, evens, turn(odds, AGG_DEV, 1)) * scale,
        jnp.where(low, turn(evens, AGG_DEV, 1), odds) * scale,
    ]

    def picked(source, at):
        return jnp.take_along_axis(source, at, axis=1, mode="promise_in_bounds")

    iterate = target
    for _ in range(CITERS - 1):
        later = []
        for c in range(2):
            rows = [
                jnp.broadcast_to(iterate[c][h : h + 1], (n_hi, 128)) for h in range(n_hi)
            ]
            value = (1.0 - OMEGA) * iterate[c] + target[c]
            for k in range(4):
                found = picked(rows[0], col_lo[k])
                for h in range(1, n_hi):
                    found = jnp.where(col_hi[k] == h, picked(rows[h], col_lo[k]), found)
                value = value - weights[k] * found
            later.append(value)
        iterate = later
    xs[0] = iterate[0]
    xs[1] = iterate[1]

    def corrected(owner, at):
        h = lax.div(owner, 2)
        source = jnp.where(
            sub < 4,
            jnp.broadcast_to(xs[0, pl.ds(h, 1), :], (8, 128)),
            jnp.broadcast_to(xs[1, pl.ds(h, 1), :], (8, 128)),
        )
        return picked(source, at + AGG_DEV * lax.rem(owner, 2))

    edge_agg = edge.astype(I32)
    agg_left = jnp.broadcast_to(edge_agg[:, 42:43], (8, 128))
    agg_right = jnp.broadcast_to(edge_agg[:, 41:42], (8, 128))
    corr = corrected(py, agg_own)
    corr_edge = jnp.where(
        lane < 64,
        corrected(wrap(py - 1, n_py), agg_left),
        corrected(wrap(py + 1, n_py), agg_right),
    )
    half = lane >> 6
    corr_edge = jnp.where((half != no_left) & (half != no_right), corr_edge, 0.0)
    ct[0] = corr
    ct[1] = corr_edge

    round4 = [send(ct, cr.at[0], peer(1, 0)), send(ct, cr.at[1], peer(-1, 0))]
    for copy in round4:
        copy.wait_recv()

    def rows_joined(i, own):
        joined = jnp.where(
            row == 0, turn(cr[0, i], -2, 0), jnp.where(row == 3, turn(cr[1, i], 2, 0), own)
        )
        return jnp.where(row_ok, joined, 0.0)

    corr_beside = beside(rows_joined(0, corr), rows_joined(1, corr_edge))
    result = ans[...]
    for d, (dx, dy) in enumerate(OFFSETS):
        result = result + ws[:, d] * turn(corr_beside[dy + 1], -dx, 0)
    ans[...] = result
    for copy in round1 + round2 + round3 + round4:
        copy.wait_send()


def write_out(image, answer, image_out, answer_out, sems):
    copies = []
    for c in range(2):
        rows = pl.ds(4 * c + 1, 2)
        copies.append(pltpu.make_async_copy(image.at[:, rows], image_out.at[c], sems.at[c]))
        copies.append(pltpu.make_async_copy(answer.at[:, rows], answer_out.at[c], sems.at[2 + c]))
    for copy in copies:
        copy.start()
    for copy in copies:
        copy.wait()


def solution(mesh):
    n_px, n_py = mesh.shape["px"], mesh.shape["py"]
    n_hi = n_py // 2
    n_sends = 10 + 10 + (n_py - 1) + 2

    def body(
        velocity, direction, forcing, softness, friction, links, aggregate, diag, vals, cols
    ):
        block = jax.ShapeDtypeStruct(velocity.shape, F32)
        wide = jax.ShapeDtypeStruct((LAYERS, 8, 128), F32)
        results = pl.pallas_call(
            functools.partial(kernel, n_px, n_py),
            out_shape=(wide, wide),
            in_specs=[pl.BlockSpec(memory_space=pltpu.HBM)] * 10,
            out_specs=[pl.BlockSpec(memory_space=pltpu.VMEM)] * 2,
            scratch_shapes=[
                pltpu.VMEM((2 * LAYERS + 1, 8, 128), F32),
                pltpu.VMEM((2 * LAYERS + 1, 8, 128), F32),
                pltpu.VMEM((LAYERS, 8, 128), F32),
                pltpu.VMEM((8, 128), F32),
                pltpu.VMEM((4, 8, 128), I32),
                pltpu.VMEM((8, 128), I32),
                pltpu.VMEM((n_hi, 128), F32),
                pltpu.VMEM((4, n_hi, 128), F32),
                pltpu.VMEM((4, n_hi, 128), I32),
                pltpu.VMEM((8, 128), F32),
                pltpu.VMEM((6, 8, 128), F32),
                pltpu.VMEM((LAYERS, 8, 128), F32),
                pltpu.VMEM((LAYERS, 8, 128), F32),
                pltpu.VMEM((8, 128), F32),
                pltpu.VMEM((6, 8, 128), F32),
                pltpu.VMEM((1, 1, 128), F32),
                pltpu.VMEM((n_py, 1, 128), F32),
                pltpu.VMEM((2, n_hi, 128), F32),
                pltpu.VMEM((2, 8, 128), F32),
                pltpu.VMEM((2, 2, 8, 128), F32),
                pltpu.VMEM((8, LAYERS, 8, 128), F32),
                pltpu.VMEM((8, LAYERS, 8, 128), F32),
                pltpu.VMEM((LAYERS, 8, 8, 128), F32),
                pltpu.SemaphoreType.DMA((23,)),
                pltpu.SemaphoreType.DMA((n_sends,)),
                pltpu.SemaphoreType.DMA((n_sends,)),
                pltpu.SemaphoreType.REGULAR((2,)),
            ],
            compiler_params=pltpu.CompilerParams(
                collective_id=0, has_side_effects=True, vmem_limit_bytes=32 * 1024 * 1024
            ),
        )(
            *(
                pltpu.with_memory_space_constraint(a, pltpu.HBM)
                for a in (
                    velocity,
                    direction,
                    forcing,
                    softness,
                    friction,
                    links,
                    aggregate,
                    diag.reshape(n_hi, 128),
                    vals.reshape(4, n_hi, 128).transpose(1, 0, 2),
                    cols.reshape(4, n_hi, 128).transpose(1, 0, 2),
                )
            )
        )
        return pl.pallas_call(
            write_out,
            out_shape=(block, block),
            in_specs=[pl.BlockSpec(memory_space=pl.ANY)] * 2,
            out_specs=[pl.BlockSpec(memory_space=pltpu.HBM)] * 2,
            scratch_shapes=[pltpu.SemaphoreType.DMA((4,))],
            compiler_params=pltpu.CompilerParams(vmem_limit_bytes=8 * 1024 * 1024),
        )(*results)

    return jax.shard_map(
        body,
        mesh=mesh,
        in_specs=(
            P(None, None, "px", "py"),
            P(None, None, "px", "py"),
            P(None, None, "px", "py"),
            P("px", "py"),
            P("px", "py"),
            P(None, "px", "py"),
            P("px", "py"),
            P("px"),
            P(None, "px"),
            P(None, "px"),
        ),
        out_specs=(P(None, None, "px", "py"), P(None, None, "px", "py")),
        check_vma=False,
    )
```

```python
import functools

import jax
import jax.numpy as jnp
from jax import lax
from jax.experimental import pallas as pl
from jax.experimental.pallas import tpu as pltpu
from jax.sharding import PartitionSpec as P

CITERS = 4
AGG_DEV = 64
KZ = 4.0
EPS0 = 0.05
OMEGA = 0.8
OFFSETS = ((-1, -1), (-1, 0), (-1, 1), (0, -1), (0, 1), (1, -1), (1, 0), (1, 1))
MESH = pl.DeviceIdType.MESH
LAYERS = 20
F32 = jnp.float32
I32 = jnp.int32

FIELD = 64
REACH = 4
V, X, RATE, LOAD, RUB, SLOT, AGG = 0, LAYERS, 2 * LAYERS, 2 * LAYERS + 1, 61, 62, 66
FAR, PLANES = 2 * LAYERS + 1, 67


def turn(x, shift, axis):
    shift %= x.shape[axis]
    return pltpu.roll(x, shift, axis) if shift else x


def stacked(tiles):
    return jnp.concatenate([t[None] for t in tiles], axis=0)


def vertical(x):
    return jnp.concatenate([x[1:], x[-1:]], axis=0) - jnp.concatenate([x[:1], x[:-1]], axis=0)


def kernel(
    n_px,
    n_py,
    velocity,
    direction,
    forcing,
    softness,
    friction,
    links,
    aggregate,
    coarse_diag,
    coarse_vals,
    coarse_cols,
    img,
    ans,
    own,
    near,
    far,
    lk,
    ag,
    dg,
    cv,
    cc,
    edge_send,
    edge_recv,
    rs,
    rr,
    xs,
    ct,
    cr,
    cs,
    ds_,
    ws,
    load_sem,
    send_sem,
    recv_sem,
    relay,
):
    px = lax.axis_index("px")
    py = lax.axis_index("py")
    n_hi = n_py // 2

    def wrap(value, count):
        return lax.rem(value + count, count)

    def peer(dx, dy):
        return (wrap(px + dx, n_px), wrap(py + dy, n_py))

    around = [peer(dx, dy) for dx in (-1, 1) for dy in (-1, 1, 0)]
    peers = around + [peer(0, k) for k in range(1, n_py) if min(k, n_py - k) <= REACH]
    barrier = pltpu.get_barrier_semaphore()
    for target in peers:
        pl.semaphore_signal(barrier, inc=1, device_id=target, device_id_type=MESH)
    relayed = n_py // 2 > REACH

    loads = []

    def load(src, dst):
        copy = pltpu.make_async_copy(src, dst, load_sem.at[len(loads)])
        copy.start()
        loads.append(copy)

    for c in range(2):
        rows = pl.ds(4 * c + 1, 2)
        load(velocity.at[c], own.at[pl.ds(V, LAYERS), rows])
        load(direction.at[c], own.at[pl.ds(X, LAYERS), rows])
        load(softness, own.at[RATE, rows])
        load(forcing.at[c], own.at[pl.ds(LOAD, LAYERS), rows])
        load(friction, own.at[RUB, rows])
        load(links, lk.at[:, rows])
        load(aggregate, ag.at[rows])
    first_loads = len(loads)
    load(coarse_diag, dg)
    for k in range(4):
        load(coarse_vals.at[:, k], cv.at[k])
        load(coarse_cols.at[:, k], cc.at[k])

    lane = lax.broadcasted_iota(I32, (8, 128), 1)
    sub = lax.broadcasted_iota(I32, (8, 128), 0)
    row = sub & 3
    core = (row == 1) | (row == 2)
    none = 9
    no_below = jnp.where(px > 0, none, 0)
    no_above = jnp.where(px < n_px - 1, none, 3)
    row_ok = (row != no_below) & (row != no_above)
    far_ok = row_ok & ((row == 0) | (row == 3))
    even = (lane & 1) == 0
    no_left = jnp.where(py > 0, none, 0)
    no_right = jnp.where(py < n_py - 1, none, 1)
    side_ok = ((lane & 1) != no_left) & ((lane & 1) != no_right)
    half = lane >> 6
    half_ok = (half != no_left) & (half != no_right)

    count = [0]

    def send(src, dst, target):
        i = count[0]
        count[0] += 1
        copy = pltpu.make_async_remote_copy(
            src_ref=src,
            dst_ref=dst,
            send_sem=send_sem.at[i],
            recv_sem=recv_sem.at[i],
            device_id=target,
            device_id_type=MESH,
        )
        copy.start()
        return copy

    def packed(fields, shift, gap):
        tile = jnp.zeros((8, 128), F32)
        for x, at in fields:
            put = (lane == at % 128) | (lane == (at + gap) % 128)
            tile = jnp.where(put, turn(x, at + shift, 1), tile)
        return tile

    def unpacked(tile):
        return stacked([turn(tile, -(FIELD + 2 * layer), 1) for layer in range(LAYERS)])

    def beside(x, ends):
        left = jnp.where(lane == 0, ends, turn(x, 1, x.ndim - 1))
        right = jnp.where(lane == 127, ends, turn(x, -1, x.ndim - 1))
        return left, x, right

    for copy in loads[:first_loads]:
        copy.wait()
    agg_own = jnp.where(core, ag[...], 0)
    own[AGG] = agg_own.astype(F32)
    for k in range(4):
        own[SLOT + k] = jnp.where(core, lk[k], 8).astype(F32)
    moving = [(own[V + i], 2 * i) for i in range(LAYERS)]
    moving += [(own[X + i], FIELD + 2 * i) for i in range(LAYERS)]
    moving += [(own[RATE], 2 * LAYERS)]
    fixed = [(own[AGG], 42), (own[RUB], 44)] + [(own[SLOT + k], 46 + 2 * k) for k in range(4)]
    edge_send[0] = packed(moving + fixed, 1, 1)
    edge_send[1] = packed(moving, 2, 3)
    edge_send[2] = packed([(own[LOAD + i], FIELD + 2 * i) for i in range(LAYERS)], 1, 1)
    pl.semaphore_wait(barrier, len(peers))
    if relayed:
        for k in (REACH, n_py - REACH):
            pl.semaphore_signal(relay, inc=1, device_id=peer(0, k), device_id_type=MESH)
    slot = {(dx, dy): 3 * (dy > 0) + dx + 1 for dx in (-1, 0, 1) for dy in (-1, 1)}
    round1 = []
    for dx in (-1, 1):
        for dy in (-1, 1):
            round1.append(send(edge_send, edge_recv.at[slot[-dx, -dy]], peer(dx, dy)))
    for c in range(2):
        low, high = 4 * c + 1, 4 * c + 2
        for dx, first, second, to in ((1, high, low, 4 * c), (-1, low, high, 4 * c + 3)):
            there = pl.ds(to, 1)
            round1.append(send(own.at[:, pl.ds(first, 1)], near.at[:, there], peer(dx, 0)))
            moved = own.at[pl.ds(0, FAR), pl.ds(second, 1)]
            round1.append(send(moved, far.at[:, there], peer(dx, 0)))
    for dy in (-1, 1):
        round1.append(send(edge_send, edge_recv.at[slot[0, -dy]], peer(0, dy)))

    for copy in loads[first_loads:]:
        copy.wait()
    scale = OMEGA / dg[...]
    weights = [cv[k] * scale for k in range(4)]
    cols = [cc[k] for k in range(4)]
    col_hi = [c >> 7 for c in cols]
    col_lo = [c & 127 for c in cols]
    agg_rows = [agg_own[r : r + 1, :] for r in (1, 2)]
    ids = lax.broadcasted_iota(I32, (128, 128), 0) & (AGG_DEV - 1)
    hot = [(ids == a).astype(F32) for a in agg_rows]

    for copy in round1:
        copy.wait_recv()

    def joined(first, size):
        here = jnp.where(core, own[first : first + size], near[first : first + size])
        return jnp.where(row_ok, here, 0.0)

    def outer(first, size):
        return jnp.where(far_ok, far[first : first + size], 0.0)

    def edges(i):
        shift = -4 if i == 1 else -2

        def both(column):
            left, right = column(0), column(3)
            return jnp.where(side_ok, jnp.where(even, left, turn(right, shift, 1)), 0.0)

        def inner_rows(first):
            below, here, above = (edge_recv[first + j, i] for j in range(3))
            return jnp.where(
                row == 0, turn(below, -2, 0), jnp.where(row == 3, turn(above, 2, 0), here)
            )

        def outer_rows(first):
            below, above = edge_recv[first, i], edge_recv[first + 2, i]
            return jnp.where(row == 0, turn(below, -1, 0), turn(above, 1, 0))

        return (
            jnp.where(row_ok, both(inner_rows), 0.0),
            jnp.where(far_ok, both(outer_rows), 0.0) if i < 2 else None,
        )

    top = (lane == 38) | (lane == 37) | (lane == 102) | (lane == 101)
    bottom = (lane == 0) | (lane == 127) | (lane == 64) | (lane == 63)

    def edge_vertical(tile):
        return jnp.where(top, tile, turn(tile, -2, 1)) - jnp.where(bottom, tile, turn(tile, 2, 1))

    def viscosity(shear, soft):
        axis = shear.ndim - 2
        square = shear * shear
        strain = EPS0 + 0.25 * KZ * (square + turn(square, 4, axis))
        eta = soft * jnp.exp(jnp.log(strain) * (-1.0 / 3.0))
        slope = (-2.0 / 3.0 * 0.25 * KZ) * eta / strain * shear
        return eta, slope

    def derived(slope, shear):
        rise = slope * shear
        return rise + turn(rise, 4, rise.ndim - 2)

    def state(v, x, rate):
        eta, slope = viscosity(vertical(v), rate)
        return (eta, v, x, derived(slope, vertical(x))), slope

    def edge_state(tile):
        shear = edge_vertical(tile)
        eta, slope = viscosity(shear, jnp.where(even, tile[:, 40:41], tile[:, 39:40]))
        slope = turn(slope, FIELD, 1)
        return (turn(eta, FIELD, 1), turn(tile, FIELD, 1), tile, derived(slope, shear)), slope

    def inside(v, x, rate):
        fields = [(v[i], 2 * i) for i in range(LAYERS)]
        fields += [(x[i], FIELD + 2 * i) for i in range(LAYERS)] + [(rate[0], 2 * LAYERS)]
        return packed(fields, 0, -1)

    halo = (joined(V, LAYERS), joined(X, LAYERS), joined(RATE, 1))
    rim = (outer(V, LAYERS), outer(X, LAYERS), outer(RATE, 1))
    here, slope = state(*halo)
    rim_here, _ = state(*rim)
    edge0, rim_edge0 = edges(0)
    edge1, rim_edge1 = edges(1)
    edge_load, _ = edges(2)
    at_edge, edge_slope = edge_state(edge0)
    rim_at_edge, _ = edge_state(rim_edge0)
    past_edge, _ = edge_state(edge1)
    rim_past_edge, _ = edge_state(rim_edge1)
    in_edge, _ = edge_state(inside(*halo))
    rim_in_edge, _ = edge_state(inside(*rim))

    def triples(states, ends):
        found = [beside(a, unpacked(e)) for a, e in zip(states, ends)]
        return [tuple(f[i] for f in found) for i in range(3)]

    def edge_triples(past, at, within):
        left = tuple(jnp.where(even, a, b) for a, b in zip(past, within))
        right = tuple(jnp.where(even, b, a) for a, b in zip(past, within))
        return [left, at, right]

    def halves_of(slots):
        found = []
        for d in range(len(OFFSETS)):
            tally = (slots[0] == d).astype(F32)
            for other in slots[1:]:
                tally = tally + (other == d).astype(F32)
            found.append(0.5 * tally)
        return found

    def coupling(halves, centre, around, beyond, keep):
        eta, v = centre[:2]
        axis = eta.ndim - 2
        side = pull = part = 0.0
        for dx in (-1, 0, 1):
            eta_here, v_here = turn(eta, dx, axis), turn(v, dx, axis)
            sums = [0.0, 0.0, 0.0]
            for d, (ox, oy) in enumerate(OFFSETS):
                if ox != dx:
                    continue
                weight = turn(halves[d], dx, 0)
                if dx != 0:
                    weight = jnp.where(row == (3 if dx < 0 else 0), 0.0, weight)
                eta_n, v_n, x_n, deta_n = around[oy + 1]
                couple = weight * (eta_here + eta_n)
                drop = weight * (v_here - v_n)
                if keep:
                    cs[d] = couple
                    ds_[d] = drop
                sums = [sums[0] + couple, sums[1] + drop, sums[2] + (drop * deta_n - couple * x_n)]
            side, pull, part = (
                old + turn(new, -dx, axis) for old, new in zip((side, pull, part), sums)
            )
        for oy in (-1, 0, 1):
            weight = jnp.where(row == 0, halves[OFFSETS.index((-1, oy))], 0.0)
            weight = jnp.where(row == 3, halves[OFFSETS.index((1, oy))], weight)
            eta_n, v_n, x_n, deta_n = beyond[oy + 1]
            couple = weight * (eta + eta_n)
            drop = weight * (v - v_n)
            side, pull = side + couple, pull + drop
            part = part + (drop * deta_n - couple * x_n)
        return side, pull, part

    eta, v, x, deta = here
    links_here = jnp.where(core, own[SLOT : SLOT + 4], near[SLOT : SLOT + 4])
    rub = jnp.where(core, own[RUB], near[RUB])
    side, pull, part = coupling(
        halves_of([links_here[k] for k in range(4)]),
        here,
        triples(here, at_edge),
        triples(rim_here, rim_at_edge),
        True,
    )
    face = (0.5 * KZ) * (eta[:-1] + eta[1:])
    jump = (0.5 * KZ) * (v[1:] - v[:-1])

    def column_terms(x, deta):
        flux = face * (x[1:] - x[:-1]) + jump * (deta[1:] + deta[:-1])
        return jnp.concatenate([rub * x[:1] - flux[:1], flux[:-1] - flux[1:], flux[-1:]])

    image = side * x + pull * deta + part + column_terms(x, deta)
    img[...] = image
    resid = joined(LOAD, LAYERS) - image

    def of_edge(at):
        return jnp.where(even, edge0[:, at : at + 1], edge0[:, at - 1 : at])

    edge_side, edge_pull, edge_part = coupling(
        halves_of([of_edge(46 + 2 * k) for k in range(4)]),
        at_edge,
        edge_triples(past_edge, at_edge, in_edge),
        edge_triples(rim_past_edge, rim_at_edge, rim_in_edge),
        False,
    )
    eta_e, v_e, x_e, deta_e = at_edge
    edge_rub = of_edge(44)

    def upper_of(tile):
        return turn(tile, -2, 1)

    edge_face = jnp.where(top, 0.0, (0.5 * KZ) * (eta_e + upper_of(eta_e)))
    edge_jump = (0.5 * KZ) * (upper_of(v_e) - v_e)
    flux = edge_face * (upper_of(x_e) - x_e) + edge_jump * (upper_of(deta_e) + deta_e)
    flux = jnp.where(top, 0.0, flux)
    edge_image = edge_side * x_e + edge_pull * deta_e + edge_part - flux
    edge_image = edge_image + jnp.where(bottom, edge_rub * x_e, turn(flux, 2, 1))
    edge_resid = unpacked(edge_load - edge_image)

    side2 = [stacked(pair) for pair in zip(side, unpacked(edge_side))]
    face2 = [stacked(pair) for pair in zip(face, unpacked(edge_face))]
    ends_rub = jnp.where(lane < 64, edge0[:, 44:45], edge0[:, 43:44])
    inverse2, lower2, upper2 = [], [], []
    for layer in range(LAYERS):
        pivot = side2[layer]
        if layer == 0:
            pivot = pivot + stacked([rub, ends_rub]) + face2[0]
        else:
            pivot = pivot + face2[layer - 1] - face2[layer - 1] * upper2[layer - 1]
            if layer < LAYERS - 1:
                pivot = pivot + face2[layer]
        inv = 1.0 / pivot
        inverse2.append(inv)
        lower2.append(face2[layer - 1] * inv if layer else None)
        upper2.append(face2[layer] * inv if layer < LAYERS - 1 else None)

    def line_solve(rhs, inverse, lower, upper):
        forward = [rhs[0] * inverse[0]]
        for layer in range(1, LAYERS):
            forward.append(rhs[layer] * inverse[layer] + lower[layer] * forward[-1])
        back = [forward[-1]]
        for layer in range(LAYERS - 2, -1, -1):
            back.append(forward[layer] + upper[layer] * back[-1])
        return back[::-1]

    solved = line_solve([stacked(p) for p in zip(resid, edge_resid)], inverse2, lower2, upper2)
    inverse = [a[0] for a in inverse2]
    lower = [a if a is None else a[0] for a in lower2]
    upper = [a if a is None else a[0] for a in upper2]
    smooth = jnp.where(row_ok, stacked([a[0] for a in solved]), 0.0)
    ends = jnp.where(row_ok & half_ok, stacked([a[1] for a in solved]), 0.0)

    dsmooth = derived(slope, vertical(smooth))
    dends = derived(unpacked(edge_slope), vertical(ends))
    smooth_beside = beside(smooth, ends)
    dsmooth_beside = beside(dsmooth, dends)
    after = resid - (side * smooth + pull * dsmooth + column_terms(smooth, dsmooth))
    for dx in (-1, 0, 1):
        part = 0.0
        for d, (ox, oy) in enumerate(OFFSETS):
            if ox == dx:
                part = part + (cs[d] * smooth_beside[oy + 1] - ds_[d] * dsmooth_beside[oy + 1])
        after = after + turn(part, -dx, 1)
    mean = jnp.where(core, jnp.sum(after, axis=0) / LAYERS, 0.0)

    sums = [
        lax.dot_general(
            mean, h, (((1,), (1,)), ((), ())),
            precision=lax.Precision.HIGHEST, preferred_element_type=F32,
        )
        for h in hot
    ]
    first = sums[0][1:2] + sums[1][2:3]
    second = sums[0][5:6] + sums[1][6:7]
    mine = jnp.where(lane[0:1] < AGG_DEV, first, second)
    rs[0] = mine
    if relayed:
        pl.semaphore_wait(relay, 2)
    place = lax.rem(py, 2) * n_hi + lax.div(py, 2)
    round3 = []
    for k in sorted(range(1, n_py), key=lambda k: -min(k, n_py - k)):
        round3.append(send(rs, rr.at[pl.ds(place, 1)], peer(0, k)))
    rr[place] = mine

    for d, (dx, _) in enumerate(OFFSETS):
        ws[:, d] = turn(cs[d], -dx, 1)
    rest = line_solve([after[layer] for layer in range(LAYERS)], inverse, lower, upper)
    for layer in range(LAYERS):
        ans[layer] = smooth[layer] + rest[layer]
    held = ws[0] * inverse[0]
    ws[0] = held
    for layer in range(1, LAYERS):
        held = ws[layer] * inverse[layer] + lower[layer] * held
        ws[layer] = held
    for layer in range(LAYERS - 2, -1, -1):
        held = ws[layer] + upper[layer] * held
        ws[layer] = held

    for copy in round3:
        copy.wait_recv()
    evens, odds = rr[0:n_hi, 0, :], rr[n_hi : 2 * n_hi, 0, :]
    low = lax.broadcasted_iota(I32, (n_hi, 128), 1) < AGG_DEV
    target = [
        jnp.where(low, evens, turn(odds, AGG_DEV, 1)) * scale,
        jnp.where(low, turn(evens, AGG_DEV, 1), odds) * scale,
    ]

    def picked(source, at):
        return jnp.take_along_axis(source, at, axis=1, mode="promise_in_bounds")

    iterate = target
    for _ in range(CITERS - 1):
        later = []
        for c in range(2):
            rows = [
                jnp.broadcast_to(iterate[c][h : h + 1], (n_hi, 128)) for h in range(n_hi)
            ]
            value = (1.0 - OMEGA) * iterate[c] + target[c]
            for k in range(4):
                found = picked(rows[0], col_lo[k])
                for h in range(1, n_hi):
                    found = jnp.where(col_hi[k] == h, picked(rows[h], col_lo[k]), found)
                value = value - weights[k] * found
            later.append(value)
        iterate = later
    xs[0] = iterate[0]
    xs[1] = iterate[1]

    def corrected(owner, at):
        h = lax.div(owner, 2)
        source = jnp.where(
            sub < 4,
            jnp.broadcast_to(xs[0, pl.ds(h, 1), :], (8, 128)),
            jnp.broadcast_to(xs[1, pl.ds(h, 1), :], (8, 128)),
        )
        return picked(source, at + AGG_DEV * lax.rem(owner, 2))

    edge_agg = edge0.astype(I32)
    agg_left = jnp.broadcast_to(edge_agg[:, 42:43], (8, 128))
    agg_right = jnp.broadcast_to(edge_agg[:, 41:42], (8, 128))
    corr = corrected(py, agg_own)
    corr_edge = jnp.where(
        lane < 64,
        corrected(wrap(py - 1, n_py), agg_left),
        corrected(wrap(py + 1, n_py), agg_right),
    )
    corr_edge = jnp.where(half_ok, corr_edge, 0.0)
    ct[0] = corr
    ct[1] = corr_edge

    round4 = [send(ct, cr.at[0], peer(1, 0)), send(ct, cr.at[1], peer(-1, 0))]
    for copy in round4:
        copy.wait_recv()

    def rows_joined(i, own):
        joined = jnp.where(
            row == 0, turn(cr[0, i], -2, 0), jnp.where(row == 3, turn(cr[1, i], 2, 0), own)
        )
        return jnp.where(row_ok, joined, 0.0)

    corr_beside = beside(rows_joined(0, corr), rows_joined(1, corr_edge))
    result = ans[...]
    for d, (dx, dy) in enumerate(OFFSETS):
        result = result + ws[:, d] * turn(corr_beside[dy + 1], -dx, 0)
    ans[...] = result
    for copy in round1 + round3 + round4:
        copy.wait_send()


def write_out(image, answer, image_out, answer_out, sems):
    copies = []
    for c in range(2):
        rows = pl.ds(4 * c + 1, 2)
        copies.append(pltpu.make_async_copy(image.at[:, rows], image_out.at[c], sems.at[c]))
        copies.append(pltpu.make_async_copy(answer.at[:, rows], answer_out.at[c], sems.at[2 + c]))
    for copy in copies:
        copy.start()
    for copy in copies:
        copy.wait()


def solution(mesh):
    n_px, n_py = mesh.shape["px"], mesh.shape["py"]
    n_hi = n_py // 2
    n_sends = 14 + (n_py - 1) + 2

    def body(
        velocity, direction, forcing, softness, friction, links, aggregate, diag, vals, cols
    ):
        block = jax.ShapeDtypeStruct(velocity.shape, F32)
        wide = jax.ShapeDtypeStruct((LAYERS, 8, 128), F32)
        results = pl.pallas_call(
            functools.partial(kernel, n_px, n_py),
            out_shape=(wide, wide),
            in_specs=[pl.BlockSpec(memory_space=pltpu.HBM)] * 10,
            out_specs=[pl.BlockSpec(memory_space=pltpu.VMEM)] * 2,
            scratch_shapes=[
                pltpu.VMEM((PLANES, 8, 128), F32),
                pltpu.VMEM((PLANES, 8, 128), F32),
                pltpu.VMEM((FAR, 8, 128), F32),
                pltpu.VMEM((4, 8, 128), I32),
                pltpu.VMEM((8, 128), I32),
                pltpu.VMEM((n_hi, 128), F32),
                pltpu.VMEM((4, n_hi, 128), F32),
                pltpu.VMEM((4, n_hi, 128), I32),
                pltpu.VMEM((3, 8, 128), F32),
                pltpu.VMEM((6, 3, 8, 128), F32),
                pltpu.VMEM((1, 1, 128), F32),
                pltpu.VMEM((n_py, 1, 128), F32),
                pltpu.VMEM((2, n_hi, 128), F32),
                pltpu.VMEM((2, 8, 128), F32),
                pltpu.VMEM((2, 2, 8, 128), F32),
                pltpu.VMEM((8, LAYERS, 8, 128), F32),
                pltpu.VMEM((8, LAYERS, 8, 128), F32),
                pltpu.VMEM((LAYERS, 8, 8, 128), F32),
                pltpu.SemaphoreType.DMA((23,)),
                pltpu.SemaphoreType.DMA((n_sends,)),
                pltpu.SemaphoreType.DMA((n_sends,)),
                pltpu.SemaphoreType.REGULAR,
            ],
            compiler_params=pltpu.CompilerParams(
                collective_id=0, has_side_effects=True, vmem_limit_bytes=32 * 1024 * 1024
            ),
        )(
            *(
                pltpu.with_memory_space_constraint(a, pltpu.HBM)
                for a in (
                    velocity,
                    direction,
                    forcing,
                    softness,
                    friction,
                    links,
                    aggregate,
                    diag.reshape(n_hi, 128),
                    vals.reshape(4, n_hi, 128).transpose(1, 0, 2),
                    cols.reshape(4, n_hi, 128).transpose(1, 0, 2),
                )
            )
        )
        return pl.pallas_call(
            write_out,
            out_shape=(block, block),
            in_specs=[pl.BlockSpec(memory_space=pl.ANY)] * 2,
            out_specs=[pl.BlockSpec(memory_space=pltpu.HBM)] * 2,
            scratch_shapes=[pltpu.SemaphoreType.DMA((4,))],
            compiler_params=pltpu.CompilerParams(vmem_limit_bytes=8 * 1024 * 1024),
        )(*results)

    return jax.shard_map(
        body,
        mesh=mesh,
        in_specs=(
            P(None, None, "px", "py"),
            P(None, None, "px", "py"),
            P(None, None, "px", "py"),
            P("px", "py"),
            P("px", "py"),
            P(None, "px", "py"),
            P("px", "py"),
            P("px"),
            P(None, "px"),
            P(None, "px"),
        ),
        out_specs=(P(None, None, "px", "py"), P(None, None, "px", "py")),
        check_vma=False,
    )
```

```python
import functools

import jax
import jax.numpy as jnp
from jax import lax
from jax.experimental import pallas as pl
from jax.experimental.pallas import tpu as pltpu
from jax.sharding import PartitionSpec as P

CITERS = 4
AGG_DEV = 64
KZ = 4.0
EPS0 = 0.05
OMEGA = 0.8
OFFSETS = ((-1, -1), (-1, 0), (-1, 1), (0, -1), (0, 1), (1, -1), (1, 0), (1, 1))
MESH = pl.DeviceIdType.MESH
LAYERS = 20
F32 = jnp.float32
I32 = jnp.int32

FIELD = 64
REACH = 4
V, X, RATE, LOAD, RUB, SLOT, AGG = 0, LAYERS, 2 * LAYERS, 2 * LAYERS + 1, 61, 62, 66
FAR, PLANES = 2 * LAYERS + 1, 67


def turn(x, shift, axis):
    shift %= x.shape[axis]
    return pltpu.roll(x, shift, axis) if shift else x


def stacked(tiles):
    return jnp.concatenate([t[None] for t in tiles], axis=0)


def vertical(x):
    return jnp.concatenate([x[1:], x[-1:]], axis=0) - jnp.concatenate([x[:1], x[:-1]], axis=0)


def kernel(
    n_px,
    n_py,
    velocity,
    direction,
    forcing,
    softness,
    friction,
    links,
    aggregate,
    coarse_diag,
    coarse_vals,
    coarse_cols,
    img,
    ans,
    own,
    near,
    far,
    lk,
    ag,
    cf,
    cc,
    cf_near,
    cc_near,
    edge_send,
    edge_recv,
    rs,
    rr,
    xs,
    cs,
    ds_,
    ws,
    load_sem,
    send_sem,
    recv_sem,
    gather_sem,
    relay,
    complete,
):
    px = lax.axis_index("px")
    py = lax.axis_index("py")
    n_hi = n_py // 2

    def wrap(value, count):
        return lax.rem(value + count, count)

    def peer(dx, dy):
        return (wrap(px + dx, n_px), wrap(py + dy, n_py))

    def inside_grid(dx, dy):
        ok = (px >= 0) if dx == 0 else (px > 0) if dx < 0 else (px < n_px - 1)
        return ok if dy == 0 else ok & ((py > 0) if dy < 0 else (py < n_py - 1))

    barrier = pltpu.get_barrier_semaphore()

    def greet(dx, dy):
        pl.semaphore_signal(barrier, inc=1, device_id=peer(dx, dy), device_id_type=MESH)

    line = [k for k in range(1, n_py) if min(k, n_py - k) <= REACH]
    expected = len(line)
    for dx in (-1, 1):
        for dy in (-1, 1, 0):
            pl.when(inside_grid(dx, dy))(functools.partial(greet, dx, dy))
            expected = expected + jnp.where(inside_grid(dx, dy), 1, 0)
    for k in line:
        greet(0, k)
    relayed = n_py // 2 > REACH

    loads = []

    def load(src, dst):
        copy = pltpu.make_async_copy(src, dst, load_sem.at[len(loads)])
        copy.start()
        loads.append(copy)

    for c in range(2):
        rows = pl.ds(4 * c + 1, 2)
        load(velocity.at[c], own.at[pl.ds(V, LAYERS), rows])
        load(direction.at[c], own.at[pl.ds(X, LAYERS), rows])
        load(softness, own.at[RATE, rows])
        load(forcing.at[c], own.at[pl.ds(LOAD, LAYERS), rows])
        load(friction, own.at[RUB, rows])
        load(links, lk.at[:, rows])
        load(aggregate, ag.at[rows])
    first_loads = len(loads)
    load(coarse_diag, cf.at[0])
    for k in range(4):
        load(coarse_vals.at[:, k], cf.at[1 + k])
        load(coarse_cols.at[:, k], cc.at[k])

    lane = lax.broadcasted_iota(I32, (8, 128), 1)
    sub = lax.broadcasted_iota(I32, (8, 128), 0)
    row = sub & 3
    core = (row == 1) | (row == 2)
    none = 9
    no_below = jnp.where(px > 0, none, 0)
    no_above = jnp.where(px < n_px - 1, none, 3)
    row_ok = (row != no_below) & (row != no_above)
    far_ok = row_ok & ((row == 0) | (row == 3))
    even = (lane & 1) == 0
    no_left = jnp.where(py > 0, none, 0)
    no_right = jnp.where(py < n_py - 1, none, 1)
    side_ok = ((lane & 1) != no_left) & ((lane & 1) != no_right)
    half = lane >> 6
    half_ok = (half != no_left) & (half != no_right)

    count = [0]

    def send(src, dst, target, step=(0, 0)):
        i = count[0]
        count[0] += 1
        copy = pltpu.make_async_remote_copy(
            src_ref=src,
            dst_ref=dst,
            send_sem=send_sem.at[i],
            recv_sem=recv_sem.at[i],
            device_id=target,
            device_id_type=MESH,
        )
        if step == (0, 0):
            copy.start()
        else:
            pl.when(inside_grid(*step))(copy.start)
        return copy, step

    def received(copies):
        for copy, (dx, dy) in copies:
            if (dx, dy) == (0, 0):
                copy.wait_recv()
            else:
                pl.when(inside_grid(-dx, -dy))(copy.wait_recv)

    def sent(copies):
        for copy, step in copies:
            if step == (0, 0):
                copy.wait_send()
            else:
                pl.when(inside_grid(*step))(copy.wait_send)

    def packed(fields, shift, gap):
        tile = jnp.zeros((8, 128), F32)
        for x, at in fields:
            put = (lane == at % 128) | (lane == (at + gap) % 128)
            tile = jnp.where(put, turn(x, at + shift, 1), tile)
        return tile

    def unpacked(tile):
        return stacked([turn(tile, -(FIELD + 2 * layer), 1) for layer in range(LAYERS)])

    def beside(x, ends):
        left = jnp.where(lane == 0, ends, turn(x, 1, x.ndim - 1))
        right = jnp.where(lane == 127, ends, turn(x, -1, x.ndim - 1))
        return left, x, right

    for copy in loads[:first_loads]:
        copy.wait()
    agg_own = jnp.where(core, ag[...], 0)
    own[AGG] = agg_own.astype(F32)
    for k in range(4):
        own[SLOT + k] = jnp.where(core, lk[k], 8).astype(F32)
    moving = [(own[V + i], 2 * i) for i in range(LAYERS)]
    moving += [(own[X + i], FIELD + 2 * i) for i in range(LAYERS)]
    moving += [(own[RATE], 2 * LAYERS)]
    fixed = [(own[AGG], 42), (own[RUB], 44)] + [(own[SLOT + k], 46 + 2 * k) for k in range(4)]
    edge_send[0] = packed(moving + fixed, 1, 1)
    edge_send[1] = packed(moving, 2, 3)
    edge_send[2] = packed([(own[LOAD + i], FIELD + 2 * i) for i in range(LAYERS)], 1, 1)
    pl.semaphore_wait(barrier, expected)
    if relayed:
        for k in (REACH, n_py - REACH):
            pl.semaphore_signal(relay, inc=1, device_id=peer(0, k), device_id_type=MESH)
    slot = {(dx, dy): 3 * (dy > 0) + dx + 1 for dx in (-1, 0, 1) for dy in (-1, 1)}
    round1 = []
    def send_round1(src, dst, dx, dy):
        round1.append(send(src, dst, peer(dx, dy), (dx, dy)))

    for dx in (-1, 1):
        for dy in (-1, 1):
            send_round1(edge_send, edge_recv.at[slot[-dx, -dy]], dx, dy)
    for c in range(2):
        low, high = 4 * c + 1, 4 * c + 2
        for dx, first, second, to in ((1, high, low, 4 * c), (-1, low, high, 4 * c + 3)):
            there = pl.ds(to, 1)
            send_round1(own.at[:, pl.ds(first, 1)], near.at[:, there], dx, 0)
            moved = own.at[pl.ds(0, FAR), pl.ds(second, 1)]
            send_round1(moved, far.at[:, there], dx, 0)
    for dy in (-1, 1):
        send_round1(edge_send, edge_recv.at[slot[0, -dy]], 0, dy)

    for copy in loads[first_loads:]:
        copy.wait()
    coarse = []
    for dx, i in ((1, 0), (-1, 1)):
        coarse.append(send(cf, cf_near.at[i], peer(dx, 0), (dx, 0)))
        coarse.append(send(cc, cc_near.at[i], peer(dx, 0), (dx, 0)))
    if relayed:
        pl.semaphore_wait(relay, 2)
    lines = 0
    for dx in (-1, 1):

        def tell(dx=dx):
            pl.semaphore_signal(complete, inc=1, device_id=peer(dx, 0), device_id_type=MESH)

        pl.when(inside_grid(dx, 0))(tell)
        lines = lines + jnp.where(inside_grid(dx, 0), 1, 0)
    agg_rows = [agg_own[r : r + 1, :] for r in (1, 2)]
    ids = lax.broadcasted_iota(I32, (128, 128), 0) & (AGG_DEV - 1)
    hot = [(ids == a).astype(F32) for a in agg_rows]

    received(round1)

    def joined(first, size):
        here = jnp.where(core, own[first : first + size], near[first : first + size])
        return jnp.where(row_ok, here, 0.0)

    def outer(first, size):
        return jnp.where(far_ok, far[first : first + size], 0.0)

    def edges(i):
        shift = -4 if i == 1 else -2

        def both(column):
            left, right = column(0), column(3)
            return jnp.where(side_ok, jnp.where(even, left, turn(right, shift, 1)), 0.0)

        def inner_rows(first):
            below, here, above = (edge_recv[first + j, i] for j in range(3))
            return jnp.where(
                row == 0, turn(below, -2, 0), jnp.where(row == 3, turn(above, 2, 0), here)
            )

        def outer_rows(first):
            below, above = edge_recv[first, i], edge_recv[first + 2, i]
            return jnp.where(row == 0, turn(below, -1, 0), turn(above, 1, 0))

        return (
            jnp.where(row_ok, both(inner_rows), 0.0),
            jnp.where(far_ok, both(outer_rows), 0.0) if i < 2 else None,
        )

    top = (lane == 38) | (lane == 37) | (lane == 102) | (lane == 101)
    bottom = (lane == 0) | (lane == 127) | (lane == 64) | (lane == 63)

    def edge_vertical(tile):
        return jnp.where(top, tile, turn(tile, -2, 1)) - jnp.where(bottom, tile, turn(tile, 2, 1))

    def viscosity(shear, soft):
        axis = shear.ndim - 2
        square = shear * shear
        strain = EPS0 + 0.25 * KZ * (square + turn(square, 4, axis))
        eta = soft * jnp.exp(jnp.log(strain) * (-1.0 / 3.0))
        slope = (-2.0 / 3.0 * 0.25 * KZ) * eta / strain * shear
        return eta, slope

    def derived(slope, shear):
        rise = slope * shear
        return rise + turn(rise, 4, rise.ndim - 2)

    def state(v, x, rate):
        eta, slope = viscosity(vertical(v), rate)
        return (eta, v, x, derived(slope, vertical(x))), slope

    def edge_state(tile):
        shear = edge_vertical(tile)
        eta, slope = viscosity(shear, jnp.where(even, tile[:, 40:41], tile[:, 39:40]))
        slope = turn(slope, FIELD, 1)
        return (turn(eta, FIELD, 1), turn(tile, FIELD, 1), tile, derived(slope, shear)), slope

    def inside(v, x, rate):
        fields = [(v[i], 2 * i) for i in range(LAYERS)]
        fields += [(x[i], FIELD + 2 * i) for i in range(LAYERS)] + [(rate[0], 2 * LAYERS)]
        return packed(fields, 0, -1)

    halo = (joined(V, LAYERS), joined(X, LAYERS), joined(RATE, 1))
    rim = (outer(V, LAYERS), outer(X, LAYERS), outer(RATE, 1))
    here, slope = state(*halo)
    rim_here, _ = state(*rim)
    edge0, rim_edge0 = edges(0)
    edge1, rim_edge1 = edges(1)
    edge_load, _ = edges(2)
    at_edge, edge_slope = edge_state(edge0)
    rim_at_edge, _ = edge_state(rim_edge0)
    past_edge, _ = edge_state(edge1)
    rim_past_edge, _ = edge_state(rim_edge1)
    in_edge, _ = edge_state(inside(*halo))
    rim_in_edge, _ = edge_state(inside(*rim))

    def triples(states, ends):
        found = [beside(a, unpacked(e)) for a, e in zip(states, ends)]
        return [tuple(f[i] for f in found) for i in range(3)]

    def edge_triples(past, at, within):
        left = tuple(jnp.where(even, a, b) for a, b in zip(past, within))
        right = tuple(jnp.where(even, b, a) for a, b in zip(past, within))
        return [left, at, right]

    def halves_of(slots):
        found = []
        for d in range(len(OFFSETS)):
            tally = (slots[0] == d).astype(F32)
            for other in slots[1:]:
                tally = tally + (other == d).astype(F32)
            found.append(0.5 * tally)
        return found

    def coupling(halves, centre, around, beyond, keep):
        eta, v = centre[:2]
        axis = eta.ndim - 2
        side = pull = part = 0.0
        for dx in (-1, 0, 1):
            eta_here, v_here = turn(eta, dx, axis), turn(v, dx, axis)
            sums = [0.0, 0.0, 0.0]
            for d, (ox, oy) in enumerate(OFFSETS):
                if ox != dx:
                    continue
                weight = turn(halves[d], dx, 0)
                if dx != 0:
                    weight = jnp.where(row == (3 if dx < 0 else 0), 0.0, weight)
                eta_n, v_n, x_n, deta_n = around[oy + 1]
                couple = weight * (eta_here + eta_n)
                drop = weight * (v_here - v_n)
                if keep:
                    cs[d] = couple
                    ds_[d] = drop
                sums = [sums[0] + couple, sums[1] + drop, sums[2] + (drop * deta_n - couple * x_n)]
            side, pull, part = (
                old + turn(new, -dx, axis) for old, new in zip((side, pull, part), sums)
            )
        for oy in (-1, 0, 1):
            weight = jnp.where(row == 0, halves[OFFSETS.index((-1, oy))], 0.0)
            weight = jnp.where(row == 3, halves[OFFSETS.index((1, oy))], weight)
            eta_n, v_n, x_n, deta_n = beyond[oy + 1]
            couple = weight * (eta + eta_n)
            drop = weight * (v - v_n)
            side, pull = side + couple, pull + drop
            part = part + (drop * deta_n - couple * x_n)
        return side, pull, part

    eta, v, x, deta = here
    links_here = jnp.where(core, own[SLOT : SLOT + 4], near[SLOT : SLOT + 4])
    rub = jnp.where(core, own[RUB], near[RUB])
    side, pull, part = coupling(
        halves_of([links_here[k] for k in range(4)]),
        here,
        triples(here, at_edge),
        triples(rim_here, rim_at_edge),
        True,
    )
    face = (0.5 * KZ) * (eta[:-1] + eta[1:])
    jump = (0.5 * KZ) * (v[1:] - v[:-1])

    def column_terms(x, deta):
        flux = face * (x[1:] - x[:-1]) + jump * (deta[1:] + deta[:-1])
        return jnp.concatenate([rub * x[:1] - flux[:1], flux[:-1] - flux[1:], flux[-1:]])

    image = side * x + pull * deta + part + column_terms(x, deta)
    img[...] = image
    resid = joined(LOAD, LAYERS) - image

    def of_edge(at):
        return jnp.where(even, edge0[:, at : at + 1], edge0[:, at - 1 : at])

    edge_side, edge_pull, edge_part = coupling(
        halves_of([of_edge(46 + 2 * k) for k in range(4)]),
        at_edge,
        edge_triples(past_edge, at_edge, in_edge),
        edge_triples(rim_past_edge, rim_at_edge, rim_in_edge),
        False,
    )
    eta_e, v_e, x_e, deta_e = at_edge
    edge_rub = of_edge(44)

    def upper_of(tile):
        return turn(tile, -2, 1)

    edge_face = jnp.where(top, 0.0, (0.5 * KZ) * (eta_e + upper_of(eta_e)))
    edge_jump = (0.5 * KZ) * (upper_of(v_e) - v_e)
    flux = edge_face * (upper_of(x_e) - x_e) + edge_jump * (upper_of(deta_e) + deta_e)
    flux = jnp.where(top, 0.0, flux)
    edge_image = edge_side * x_e + edge_pull * deta_e + edge_part - flux
    edge_image = edge_image + jnp.where(bottom, edge_rub * x_e, turn(flux, 2, 1))
    edge_resid = unpacked(edge_load - edge_image)

    side2 = [stacked(pair) for pair in zip(side, unpacked(edge_side))]
    face2 = [stacked(pair) for pair in zip(face, unpacked(edge_face))]
    ends_rub = jnp.where(lane < 64, edge0[:, 44:45], edge0[:, 43:44])
    inverse2, lower2, upper2 = [], [], []
    for layer in range(LAYERS):
        pivot = side2[layer]
        if layer == 0:
            pivot = pivot + stacked([rub, ends_rub]) + face2[0]
        else:
            pivot = pivot + face2[layer - 1] - face2[layer - 1] * upper2[layer - 1]
            if layer < LAYERS - 1:
                pivot = pivot + face2[layer]
        inv = 1.0 / pivot
        inverse2.append(inv)
        lower2.append(face2[layer - 1] * inv if layer else None)
        upper2.append(face2[layer] * inv if layer < LAYERS - 1 else None)

    def line_solve(rhs, inverse, lower, upper):
        forward = [rhs[0] * inverse[0]]
        for layer in range(1, LAYERS):
            forward.append(rhs[layer] * inverse[layer] + lower[layer] * forward[-1])
        back = [forward[-1]]
        for layer in range(LAYERS - 2, -1, -1):
            back.append(forward[layer] + upper[layer] * back[-1])
        return back[::-1]

    solved = line_solve([stacked(p) for p in zip(resid, edge_resid)], inverse2, lower2, upper2)
    inverse = [a[0] for a in inverse2]
    lower = [a if a is None else a[0] for a in lower2]
    upper = [a if a is None else a[0] for a in upper2]
    smooth = jnp.where(row_ok, stacked([a[0] for a in solved]), 0.0)
    ends = jnp.where(row_ok & half_ok, stacked([a[1] for a in solved]), 0.0)

    dsmooth = derived(slope, vertical(smooth))
    dends = derived(unpacked(edge_slope), vertical(ends))
    smooth_beside = beside(smooth, ends)
    dsmooth_beside = beside(dsmooth, dends)
    after = resid - (side * smooth + pull * dsmooth + column_terms(smooth, dsmooth))
    for dx in (-1, 0, 1):
        part = 0.0
        for d, (ox, oy) in enumerate(OFFSETS):
            if ox == dx:
                part = part + (cs[d] * smooth_beside[oy + 1] - ds_[d] * dsmooth_beside[oy + 1])
        after = after + turn(part, -dx, 1)
    mean = jnp.where(core, jnp.sum(after, axis=0) / LAYERS, 0.0)

    sums = [
        lax.dot_general(
            mean, h, (((1,), (1,)), ((), ())),
            precision=lax.Precision.HIGHEST, preferred_element_type=F32,
        )
        for h in hot
    ]
    first = sums[0][1:2] + sums[1][2:3]
    second = sums[0][5:6] + sums[1][6:7]
    mine = jnp.where(lane[0:1] < AGG_DEV, first, second)
    rs[0] = mine
    place = lax.rem(py, 2) * n_hi + lax.div(py, 2)

    def push(dx, k):
        group = 1 - dx
        pltpu.make_async_remote_copy(
            src_ref=rs,
            dst_ref=rr.at[pl.ds(group * n_py + place, 1)],
            send_sem=gather_sem.at[1 + dx],
            recv_sem=gather_sem.at[3 + group],
            device_id=peer(dx, k),
            device_id_type=MESH,
        ).start()

    pl.semaphore_wait(complete, lines)
    for reach in range(n_py // 2, -1, -1):
        far_off = sorted({reach, (n_py - reach) % n_py})
        for dx in (-1, 1):

            def push_all(dx=dx, far_off=far_off):
                for k in far_off:
                    push(dx, k)

            pl.when(inside_grid(dx, 0))(push_all)
        for k in far_off:
            if k:
                push(0, k)
    kept = pltpu.make_async_copy(rs, rr.at[pl.ds(n_py + place, 1)], gather_sem.at[4])
    kept.start()

    def gathered(sem, first, size):
        some = rr.at[pl.ds(first, size)]
        pltpu.make_async_copy(some, some, gather_sem.at[sem]).wait()

    for d, (dx, _) in enumerate(OFFSETS):
        ws[:, d] = turn(cs[d], -dx, 1)
    rest = line_solve([after[layer] for layer in range(LAYERS)], inverse, lower, upper)
    for layer in range(LAYERS):
        ans[layer] = smooth[layer] + rest[layer]
    held = ws[0] * inverse[0]
    ws[0] = held
    for layer in range(1, LAYERS):
        held = ws[layer] * inverse[layer] + lower[layer] * held
        ws[layer] = held
    for layer in range(LAYERS - 2, -1, -1):
        held = ws[layer] + upper[layer] * held
        ws[layer] = held

    received(coarse)
    operators = []
    for f, c in ((cf_near.at[0], cc_near.at[0]), (cf, cc), (cf_near.at[1], cc_near.at[1])):
        scale = OMEGA / f[0]
        cols = [c[k] for k in range(4)]
        weights = [f[1 + k] * scale for k in range(4)]
        operators.append((scale, weights, [a >> 7 for a in cols], [a & 127 for a in cols]))
    agg_all = jnp.where(core, own[AGG], near[AGG])
    agg_all = jnp.where(row_ok, agg_all, 0.0).astype(I32)
    sent(round1 + coarse)
    gathered(4, n_py, n_py)
    pl.when(inside_grid(-1, 0))(lambda: gathered(3, 0, n_py))
    pl.when(inside_grid(1, 0))(lambda: gathered(5, 2 * n_py, n_py))
    low = lax.broadcasted_iota(I32, (n_hi, 128), 1) < AGG_DEV

    def picked(source, at):
        return jnp.take_along_axis(source, at, axis=1, mode="promise_in_bounds")

    for g, (scale, weights, col_hi, col_lo) in enumerate(operators):
        evens = rr[g * n_py : g * n_py + n_hi, 0, :]
        odds = rr[g * n_py + n_hi : (g + 1) * n_py, 0, :]
        target = [
            jnp.where(low, evens, turn(odds, AGG_DEV, 1)) * scale,
            jnp.where(low, turn(evens, AGG_DEV, 1), odds) * scale,
        ]
        iterate = target
        for _ in range(CITERS - 1):
            later = []
            for c in range(2):
                rows = [
                    jnp.broadcast_to(iterate[c][h : h + 1], (n_hi, 128)) for h in range(n_hi)
                ]
                value = (1.0 - OMEGA) * iterate[c] + target[c]
                for k in range(4):
                    found = picked(rows[0], col_lo[k])
                    for h in range(1, n_hi):
                        found = jnp.where(col_hi[k] == h, picked(rows[h], col_lo[k]), found)
                    value = value - weights[k] * found
                later.append(value)
            iterate = later
        xs[g, 0] = iterate[0]
        xs[g, 1] = iterate[1]

    def corrected(owner, at):
        h = pl.ds(lax.div(owner, 2), 1)
        source = None
        for g in range(3):
            line = jnp.where(sub < 4, xs[g, 0, h, :], xs[g, 1, h, :])
            source = line if g == 0 else jnp.where(row >= (1 if g == 1 else 3), line, source)
        return picked(source, at + AGG_DEV * lax.rem(owner, 2))

    edge_agg = edge0.astype(I32)
    agg_left = jnp.broadcast_to(edge_agg[:, 42:43], (8, 128))
    agg_right = jnp.broadcast_to(edge_agg[:, 41:42], (8, 128))
    corr = jnp.where(row_ok, corrected(py, agg_all), 0.0)
    corr_edge = jnp.where(
        half == 0,
        corrected(wrap(py - 1, n_py), agg_left),
        corrected(wrap(py + 1, n_py), agg_right),
    )
    corr_edge = jnp.where(row_ok & half_ok, corr_edge, 0.0)
    corr_beside = beside(corr, corr_edge)
    result = ans[...]
    for d, (dx, dy) in enumerate(OFFSETS):
        result = result + ws[:, d] * turn(corr_beside[dy + 1], -dx, 0)
    ans[...] = result
    gathered(1, 0, n_py - 1)
    pl.when(inside_grid(-1, 0))(lambda: gathered(0, 0, n_py))
    pl.when(inside_grid(1, 0))(lambda: gathered(2, 0, n_py))


def write_out(image, answer, image_out, answer_out, sems):
    copies = []
    for c in range(2):
        rows = pl.ds(4 * c + 1, 2)
        copies.append(pltpu.make_async_copy(image.at[:, rows], image_out.at[c], sems.at[c]))
        copies.append(pltpu.make_async_copy(answer.at[:, rows], answer_out.at[c], sems.at[2 + c]))
    for copy in copies:
        copy.start()
    for copy in copies:
        copy.wait()


def solution(mesh):
    n_px, n_py = mesh.shape["px"], mesh.shape["py"]
    n_hi = n_py // 2
    n_sends = 18

    def body(
        velocity, direction, forcing, softness, friction, links, aggregate, diag, vals, cols
    ):
        block = jax.ShapeDtypeStruct(velocity.shape, F32)
        wide = jax.ShapeDtypeStruct((LAYERS, 8, 128), F32)
        results = pl.pallas_call(
            functools.partial(kernel, n_px, n_py),
            out_shape=(wide, wide),
            in_specs=[pl.BlockSpec(memory_space=pltpu.HBM)] * 10,
            out_specs=[pl.BlockSpec(memory_space=pltpu.VMEM)] * 2,
            scratch_shapes=[
                pltpu.VMEM((PLANES, 8, 128), F32),
                pltpu.VMEM((PLANES, 8, 128), F32),
                pltpu.VMEM((FAR, 8, 128), F32),
                pltpu.VMEM((4, 8, 128), I32),
                pltpu.VMEM((8, 128), I32),
                pltpu.VMEM((5, n_hi, 128), F32),
                pltpu.VMEM((4, n_hi, 128), I32),
                pltpu.VMEM((2, 5, n_hi, 128), F32),
                pltpu.VMEM((2, 4, n_hi, 128), I32),
                pltpu.VMEM((3, 8, 128), F32),
                pltpu.VMEM((6, 3, 8, 128), F32),
                pltpu.VMEM((1, 1, 128), F32),
                pltpu.VMEM((3 * n_py, 1, 128), F32),
                pltpu.VMEM((3, 2, n_hi, 128), F32),
                pltpu.VMEM((8, LAYERS, 8, 128), F32),
                pltpu.VMEM((8, LAYERS, 8, 128), F32),
                pltpu.VMEM((LAYERS, 8, 8, 128), F32),
                pltpu.SemaphoreType.DMA((23,)),
                pltpu.SemaphoreType.DMA((n_sends,)),
                pltpu.SemaphoreType.DMA((n_sends,)),
                pltpu.SemaphoreType.DMA((6,)),
                pltpu.SemaphoreType.REGULAR,
                pltpu.SemaphoreType.REGULAR,
            ],
            compiler_params=pltpu.CompilerParams(
                collective_id=0, has_side_effects=True, vmem_limit_bytes=32 * 1024 * 1024
            ),
        )(
            *(
                pltpu.with_memory_space_constraint(a, pltpu.HBM)
                for a in (
                    velocity,
                    direction,
                    forcing,
                    softness,
                    friction,
                    links,
                    aggregate,
                    diag.reshape(n_hi, 128),
                    vals.reshape(4, n_hi, 128).transpose(1, 0, 2),
                    cols.reshape(4, n_hi, 128).transpose(1, 0, 2),
                )
            )
        )
        return pl.pallas_call(
            write_out,
            out_shape=(block, block),
            in_specs=[pl.BlockSpec(memory_space=pl.ANY)] * 2,
            out_specs=[pl.BlockSpec(memory_space=pltpu.HBM)] * 2,
            scratch_shapes=[pltpu.SemaphoreType.DMA((4,))],
            compiler_params=pltpu.CompilerParams(vmem_limit_bytes=8 * 1024 * 1024),
        )(*results)

    return jax.shard_map(
        body,
        mesh=mesh,
        in_specs=(
            P(None, None, "px", "py"),
            P(None, None, "px", "py"),
            P(None, None, "px", "py"),
            P("px", "py"),
            P("px", "py"),
            P(None, "px", "py"),
            P("px", "py"),
            P("px"),
            P(None, "px"),
            P(None, "px"),
        ),
        out_specs=(P(None, None, "px", "py"), P(None, None, "px", "py")),
        check_vma=False,
    )
```

```python
import functools

import jax
import jax.numpy as jnp
from jax import lax
from jax.experimental import pallas as pl
from jax.experimental.pallas import tpu as pltpu
from jax.sharding import PartitionSpec as P

CITERS = 4
AGG_DEV = 64
KZ = 4.0
EPS0 = 0.05
OMEGA = 0.8
OFFSETS = ((-1, -1), (-1, 0), (-1, 1), (0, -1), (0, 1), (1, -1), (1, 0), (1, 1))
MESH = pl.DeviceIdType.MESH
LAYERS = 20
F32 = jnp.float32
I32 = jnp.int32

FIELD = 64
REACH = 4
V, X, RATE, LOAD, RUB, SLOT, AGG = 0, LAYERS, 2 * LAYERS, 2 * LAYERS + 1, 61, 62, 66
FAR, PLANES = 2 * LAYERS + 1, 67


def turn(x, shift, axis):
    shift %= x.shape[axis]
    return pltpu.roll(x, shift, axis) if shift else x


def stacked(tiles):
    return jnp.concatenate([t[None] for t in tiles], axis=0)


def vertical(x):
    return jnp.concatenate([x[1:], x[-1:]], axis=0) - jnp.concatenate([x[:1], x[:-1]], axis=0)


def kernel(
    n_px,
    n_py,
    velocity,
    direction,
    forcing,
    softness,
    friction,
    links,
    aggregate,
    coarse_diag,
    coarse_vals,
    coarse_cols,
    img,
    ans,
    own,
    near,
    far,
    lk,
    ag,
    cf,
    cc,
    cf_near,
    cc_near,
    edge_send,
    edge_recv,
    rs,
    rr,
    xs,
    cs,
    ds_,
    ws,
    load_sem,
    send_sem,
    recv_sem,
    gather_sem,
    relay,
    complete,
):
    px = lax.axis_index("px")
    py = lax.axis_index("py")
    n_hi = n_py // 2

    def wrap(value, count):
        return lax.rem(value + count, count)

    def peer(dx, dy):
        return (wrap(px + dx, n_px), wrap(py + dy, n_py))

    def inside_grid(dx, dy):
        ok = (px >= 0) if dx == 0 else (px > 0) if dx < 0 else (px < n_px - 1)
        return ok if dy == 0 else ok & ((py > 0) if dy < 0 else (py < n_py - 1))

    barrier = pltpu.get_barrier_semaphore()

    def greet(dx, dy):
        pl.semaphore_signal(barrier, inc=1, device_id=peer(dx, dy), device_id_type=MESH)

    line = [k for k in range(1, n_py) if min(k, n_py - k) <= REACH]
    expected = len(line)
    for dx in (-1, 1):
        for dy in (-1, 1, 0):
            pl.when(inside_grid(dx, dy))(functools.partial(greet, dx, dy))
            expected = expected + jnp.where(inside_grid(dx, dy), 1, 0)
    for k in line:
        greet(0, k)
    relayed = n_py // 2 > REACH

    loads = []

    def load(src, dst):
        copy = pltpu.make_async_copy(src, dst, load_sem.at[len(loads)])
        copy.start()
        loads.append(copy)

    for c in range(2):
        rows = pl.ds(4 * c + 1, 2)
        load(velocity.at[c], own.at[pl.ds(V, LAYERS), rows])
        load(direction.at[c], own.at[pl.ds(X, LAYERS), rows])
        load(softness, own.at[RATE, rows])
        load(forcing.at[c], own.at[pl.ds(LOAD, LAYERS), rows])
        load(friction, own.at[RUB, rows])
        load(links, lk.at[:, rows])
        load(aggregate, ag.at[rows])
    first_loads = len(loads)
    load(coarse_diag, cf.at[0])
    for k in range(4):
        load(coarse_vals.at[:, k], cf.at[1 + k])
        load(coarse_cols.at[:, k], cc.at[k])

    lane = lax.broadcasted_iota(I32, (8, 128), 1)
    sub = lax.broadcasted_iota(I32, (8, 128), 0)
    row = sub & 3
    core = (row == 1) | (row == 2)
    none = 9
    no_below = jnp.where(px > 0, none, 0)
    no_above = jnp.where(px < n_px - 1, none, 3)
    row_ok = (row != no_below) & (row != no_above)
    far_ok = row_ok & ((row == 0) | (row == 3))
    even = (lane & 1) == 0
    no_left = jnp.where(py > 0, none, 0)
    no_right = jnp.where(py < n_py - 1, none, 1)
    side_ok = ((lane & 1) != no_left) & ((lane & 1) != no_right)
    half = lane >> 6
    half_ok = (half != no_left) & (half != no_right)

    count = [0]

    def send(src, dst, target, to_ok, from_ok):
        i = count[0]
        count[0] += 1
        copy = pltpu.make_async_remote_copy(
            src_ref=src,
            dst_ref=dst,
            send_sem=send_sem.at[i],
            recv_sem=recv_sem.at[i],
            device_id=target,
            device_id_type=MESH,
        )
        pl.when(to_ok)(copy.start)
        return copy, to_ok, from_ok

    def received(copies):
        for copy, _, from_ok in copies:
            pl.when(from_ok)(copy.wait_recv)

    def sent(copies):
        for copy, to_ok, _ in copies:
            pl.when(to_ok)(copy.wait_send)

    def packed(fields, shift, gap):
        tile = jnp.zeros((8, 128), F32)
        for x, at in fields:
            put = (lane == at % 128) | (lane == (at + gap) % 128)
            tile = jnp.where(put, turn(x, at + shift, 1), tile)
        return tile

    def unpacked(tile):
        return stacked([turn(tile, -(FIELD + 2 * layer), 1) for layer in range(LAYERS)])

    def beside(x, ends):
        left = jnp.where(lane == 0, ends, turn(x, 1, x.ndim - 1))
        right = jnp.where(lane == 127, ends, turn(x, -1, x.ndim - 1))
        return left, x, right

    for copy in loads[:first_loads]:
        copy.wait()
    agg_own = jnp.where(core, ag[...], 0)
    own[AGG] = agg_own.astype(F32)
    for k in range(4):
        own[SLOT + k] = jnp.where(core, lk[k], 8).astype(F32)
    moving = [(own[V + i], 2 * i) for i in range(LAYERS)]
    moving += [(own[X + i], FIELD + 2 * i) for i in range(LAYERS)]
    moving += [(own[RATE], 2 * LAYERS)]
    fixed = [(own[AGG], 42), (own[RUB], 44)] + [(own[SLOT + k], 46 + 2 * k) for k in range(4)]
    edge_send[0] = packed(moving + fixed, 1, 1)
    edge_send[1] = packed(moving, 2, 3)
    edge_send[2] = packed([(own[LOAD + i], FIELD + 2 * i) for i in range(LAYERS)], 1, 1)
    pl.semaphore_wait(barrier, expected)
    if relayed:
        for k in (REACH, n_py - REACH):
            pl.semaphore_signal(relay, inc=1, device_id=peer(0, k), device_id_type=MESH)
    slot = {(dx, dy): 3 * (dy > 0) + dx + 1 for dx in (-1, 0, 1) for dy in (-1, 1)}
    round1 = []
    def send_round1(src, dst, dx, dy):
        to_ok, from_ok = inside_grid(dx, dy), inside_grid(-dx, -dy)
        round1.append(send(src, dst, peer(dx, dy), to_ok, from_ok))

    for dx in (-1, 1):
        for dy in (-1, 1):
            send_round1(edge_send, edge_recv.at[slot[-dx, -dy]], dx, dy)
    for c in range(2):
        low, high = 4 * c + 1, 4 * c + 2
        for dx, first, second, to in ((1, high, low, 4 * c), (-1, low, high, 4 * c + 3)):
            there = pl.ds(to, 1)
            send_round1(own.at[:, pl.ds(first, 1)], near.at[:, there], dx, 0)
            moved = own.at[pl.ds(0, FAR), pl.ds(second, 1)]
            send_round1(moved, far.at[:, there], dx, 0)
    for dy in (-1, 1):
        send_round1(edge_send, edge_recv.at[slot[0, -dy]], 0, dy)

    odd = lax.rem(px, 2)
    pairs = []
    for dx in (1 - 2 * odd, 2 * odd - 1):
        pairs.append((dx, (px + dx >= 0) & (px + dx < n_px)))
    for copy in loads[first_loads:]:
        copy.wait()
    coarse = []
    for i, (dx, ok) in enumerate(pairs):
        coarse.append(send(cf, cf_near.at[i], peer(dx, 0), ok, ok))
        coarse.append(send(cc, cc_near.at[i], peer(dx, 0), ok, ok))
    if relayed:
        pl.semaphore_wait(relay, 2)
    lines = 0
    for dx in (-1, 1):

        def tell(dx=dx):
            pl.semaphore_signal(complete, inc=1, device_id=peer(dx, 0), device_id_type=MESH)

        pl.when(inside_grid(dx, 0))(tell)
        lines = lines + jnp.where(inside_grid(dx, 0), 1, 0)
    agg_rows = [agg_own[r : r + 1, :] for r in (1, 2)]
    ids = lax.broadcasted_iota(I32, (128, 128), 0) & (AGG_DEV - 1)
    hot = [(ids == a).astype(F32) for a in agg_rows]

    received(round1)

    def joined(first, size):
        here = jnp.where(core, own[first : first + size], near[first : first + size])
        return jnp.where(row_ok, here, 0.0)

    def outer(first, size):
        return jnp.where(far_ok, far[first : first + size], 0.0)

    def edges(i):
        shift = -4 if i == 1 else -2

        def both(column):
            left, right = column(0), column(3)
            return jnp.where(side_ok, jnp.where(even, left, turn(right, shift, 1)), 0.0)

        def inner_rows(first):
            below, here, above = (edge_recv[first + j, i] for j in range(3))
            return jnp.where(
                row == 0, turn(below, -2, 0), jnp.where(row == 3, turn(above, 2, 0), here)
            )

        def outer_rows(first):
            below, above = edge_recv[first, i], edge_recv[first + 2, i]
            return jnp.where(row == 0, turn(below, -1, 0), turn(above, 1, 0))

        return (
            jnp.where(row_ok, both(inner_rows), 0.0),
            jnp.where(far_ok, both(outer_rows), 0.0) if i < 2 else None,
        )

    top = (lane == 38) | (lane == 37) | (lane == 102) | (lane == 101)
    bottom = (lane == 0) | (lane == 127) | (lane == 64) | (lane == 63)

    def edge_vertical(tile):
        return jnp.where(top, tile, turn(tile, -2, 1)) - jnp.where(bottom, tile, turn(tile, 2, 1))

    def viscosity(shear, soft):
        axis = shear.ndim - 2
        square = shear * shear
        strain = EPS0 + 0.25 * KZ * (square + turn(square, 4, axis))
        eta = soft * jnp.exp(jnp.log(strain) * (-1.0 / 3.0))
        slope = (-2.0 / 3.0 * 0.25 * KZ) * eta / strain * shear
        return eta, slope

    def derived(slope, shear):
        rise = slope * shear
        return rise + turn(rise, 4, rise.ndim - 2)

    def state(v, x, rate):
        eta, slope = viscosity(vertical(v), rate)
        return (eta, v, x, derived(slope, vertical(x))), slope

    def edge_state(tile):
        shear = edge_vertical(tile)
        eta, slope = viscosity(shear, jnp.where(even, tile[:, 40:41], tile[:, 39:40]))
        slope = turn(slope, FIELD, 1)
        return (turn(eta, FIELD, 1), turn(tile, FIELD, 1), tile, derived(slope, shear)), slope

    def inside(v, x, rate):
        fields = [(v[i], 2 * i) for i in range(LAYERS)]
        fields += [(x[i], FIELD + 2 * i) for i in range(LAYERS)] + [(rate[0], 2 * LAYERS)]
        return packed(fields, 0, -1)

    halo = (joined(V, LAYERS), joined(X, LAYERS), joined(RATE, 1))
    rim = (outer(V, LAYERS), outer(X, LAYERS), outer(RATE, 1))
    here, slope = state(*halo)
    rim_here, _ = state(*rim)
    edge0, rim_edge0 = edges(0)
    edge1, rim_edge1 = edges(1)
    edge_load, _ = edges(2)
    at_edge, edge_slope = edge_state(edge0)
    rim_at_edge, _ = edge_state(rim_edge0)
    past_edge, _ = edge_state(edge1)
    rim_past_edge, _ = edge_state(rim_edge1)
    in_edge, _ = edge_state(inside(*halo))
    rim_in_edge, _ = edge_state(inside(*rim))

    def triples(states, ends):
        found = [beside(a, unpacked(e)) for a, e in zip(states, ends)]
        return [tuple(f[i] for f in found) for i in range(3)]

    def edge_triples(past, at, within):
        left = tuple(jnp.where(even, a, b) for a, b in zip(past, within))
        right = tuple(jnp.where(even, b, a) for a, b in zip(past, within))
        return [left, at, right]

    def halves_of(slots):
        found = []
        for d in range(len(OFFSETS)):
            tally = (slots[0] == d).astype(F32)
            for other in slots[1:]:
                tally = tally + (other == d).astype(F32)
            found.append(0.5 * tally)
        return found

    def coupling(halves, centre, around, beyond, keep):
        eta, v = centre[:2]
        axis = eta.ndim - 2
        side = pull = part = 0.0
        for dx in (-1, 0, 1):
            eta_here, v_here = turn(eta, dx, axis), turn(v, dx, axis)
            sums = [0.0, 0.0, 0.0]
            for d, (ox, oy) in enumerate(OFFSETS):
                if ox != dx:
                    continue
                weight = turn(halves[d], dx, 0)
                if dx != 0:
                    weight = jnp.where(row == (3 if dx < 0 else 0), 0.0, weight)
                eta_n, v_n, x_n, deta_n = around[oy + 1]
                couple = weight * (eta_here + eta_n)
                drop = weight * (v_here - v_n)
                if keep:
                    cs[d] = couple
                    ds_[d] = drop
                sums = [sums[0] + couple, sums[1] + drop, sums[2] + (drop * deta_n - couple * x_n)]
            side, pull, part = (
                old + turn(new, -dx, axis) for old, new in zip((side, pull, part), sums)
            )
        for oy in (-1, 0, 1):
            weight = jnp.where(row == 0, halves[OFFSETS.index((-1, oy))], 0.0)
            weight = jnp.where(row == 3, halves[OFFSETS.index((1, oy))], weight)
            eta_n, v_n, x_n, deta_n = beyond[oy + 1]
            couple = weight * (eta + eta_n)
            drop = weight * (v - v_n)
            side, pull = side + couple, pull + drop
            part = part + (drop * deta_n - couple * x_n)
        return side, pull, part

    eta, v, x, deta = here
    links_here = jnp.where(core, own[SLOT : SLOT + 4], near[SLOT : SLOT + 4])
    rub = jnp.where(core, own[RUB], near[RUB])
    side, pull, part = coupling(
        halves_of([links_here[k] for k in range(4)]),
        here,
        triples(here, at_edge),
        triples(rim_here, rim_at_edge),
        True,
    )
    face = (0.5 * KZ) * (eta[:-1] + eta[1:])
    jump = (0.5 * KZ) * (v[1:] - v[:-1])

    def column_terms(x, deta):
        flux = face * (x[1:] - x[:-1]) + jump * (deta[1:] + deta[:-1])
        return jnp.concatenate([rub * x[:1] - flux[:1], flux[:-1] - flux[1:], flux[-1:]])

    image = side * x + pull * deta + part + column_terms(x, deta)
    img[...] = image
    resid = joined(LOAD, LAYERS) - image

    def of_edge(at):
        return jnp.where(even, edge0[:, at : at + 1], edge0[:, at - 1 : at])

    edge_side, edge_pull, edge_part = coupling(
        halves_of([of_edge(46 + 2 * k) for k in range(4)]),
        at_edge,
        edge_triples(past_edge, at_edge, in_edge),
        edge_triples(rim_past_edge, rim_at_edge, rim_in_edge),
        False,
    )
    eta_e, v_e, x_e, deta_e = at_edge
    edge_rub = of_edge(44)

    def upper_of(tile):
        return turn(tile, -2, 1)

    edge_face = jnp.where(top, 0.0, (0.5 * KZ) * (eta_e + upper_of(eta_e)))
    edge_jump = (0.5 * KZ) * (upper_of(v_e) - v_e)
    flux = edge_face * (upper_of(x_e) - x_e) + edge_jump * (upper_of(deta_e) + deta_e)
    flux = jnp.where(top, 0.0, flux)
    edge_image = edge_side * x_e + edge_pull * deta_e + edge_part - flux
    edge_image = edge_image + jnp.where(bottom, edge_rub * x_e, turn(flux, 2, 1))
    edge_resid = unpacked(edge_load - edge_image)

    side2 = [stacked(pair) for pair in zip(side, unpacked(edge_side))]
    face2 = [stacked(pair) for pair in zip(face, unpacked(edge_face))]
    ends_rub = jnp.where(lane < 64, edge0[:, 44:45], edge0[:, 43:44])
    middle = LAYERS // 2
    inverse2, inward2, outward2 = [None] * LAYERS, [None] * LAYERS, [None] * LAYERS

    def eliminate(layer, before, after):
        pivot = side2[layer]
        if layer == 0:
            pivot = pivot + stacked([rub, ends_rub])
        if after is not None:
            pivot = pivot + face2[after]
        if before is not None:
            previous = layer - 1 if layer < middle else layer + 1
            pivot = pivot + face2[before] - face2[before] * outward2[previous]
        inv = 1.0 / pivot
        inverse2[layer] = inv
        inward2[layer] = None if before is None else face2[before] * inv
        outward2[layer] = None if after is None else face2[after] * inv

    for step in range(middle):
        eliminate(step, step - 1 if step else None, step)
        layer = LAYERS - 1 - step
        eliminate(layer, layer if step else None, layer - 1)
    meet2 = 1.0 / (1.0 - outward2[middle - 1] * outward2[middle])

    def line_solve(rhs, inverse, inward, outward, meet):
        found = [None] * LAYERS
        for step in range(middle):
            for layer, previous in ((step, step - 1), (LAYERS - 1 - step, LAYERS - step)):
                found[layer] = rhs[layer] * inverse[layer]
                if step:
                    found[layer] = found[layer] + inward[layer] * found[previous]
        low, high = middle - 1, middle
        found[low] = (found[low] + outward[low] * found[high]) * meet
        found[high] = found[high] + outward[high] * found[low]
        for step in range(1, middle):
            for layer, previous in ((low - step, low - step + 1), (high + step, high + step - 1)):
                found[layer] = found[layer] + outward[layer] * found[previous]
        return found

    solved = line_solve(
        [stacked(p) for p in zip(resid, edge_resid)], inverse2, inward2, outward2, meet2
    )
    own_factors = [
        [a if a is None else a[0] for a in factor] for factor in (inverse2, inward2, outward2)
    ] + [meet2[0]]
    smooth = jnp.where(row_ok, stacked([a[0] for a in solved]), 0.0)
    ends = jnp.where(row_ok & half_ok, stacked([a[1] for a in solved]), 0.0)

    dsmooth = derived(slope, vertical(smooth))
    dends = derived(unpacked(edge_slope), vertical(ends))
    smooth_beside = beside(smooth, ends)
    dsmooth_beside = beside(dsmooth, dends)
    plain = resid - (side * smooth + pull * dsmooth)
    parts = []
    for dx in (-1, 0, 1):
        part = 0.0
        for d, (ox, oy) in enumerate(OFFSETS):
            if ox == dx:
                part = part + (cs[d] * smooth_beside[oy + 1] - ds_[d] * dsmooth_beside[oy + 1])
        parts.append(part)
    total = jnp.sum(plain, axis=0) - rub * smooth[0]
    for dx, part in zip((-1, 0, 1), parts):
        total = total + turn(jnp.sum(part, axis=0), -dx, 0)
    mean = jnp.where(core, total / LAYERS, 0.0)

    pieces, rest_of = [], mean
    for _ in range(2):
        large = rest_of * 65537.0
        piece = large - (large - rest_of)
        pieces.append(piece)
        rest_of = rest_of - piece
    pieces.append(rest_of)
    pieces = jnp.concatenate(pieces, axis=0)
    sums = lax.dot_general(
        jnp.concatenate([pieces, turn(pieces, -1, 0)], axis=1),
        jnp.concatenate(hot, axis=1),
        (((1,), (1,)), ((), ())),
        preferred_element_type=F32,
    )
    sums = sums[0:8] + sums[8:16] + sums[16:24]
    mine = jnp.where(lane[0:1] < AGG_DEV, sums[1:2], sums[5:6])
    rs[0] = mine
    place = lax.rem(py, 2) * n_hi + lax.div(py, 2)

    def push(group, dx, k):
        pltpu.make_async_remote_copy(
            src_ref=rs,
            dst_ref=rr.at[pl.ds(group * n_py + place, 1)],
            send_sem=gather_sem.at[group],
            recv_sem=gather_sem.at[3 + group],
            device_id=peer(dx, k),
            device_id_type=MESH,
        ).start()

    pl.semaphore_wait(complete, lines)
    for reach in range(n_py // 2, -1, -1):
        far_off = sorted({reach, (n_py - reach) % n_py})
        for group in (2, 1):
            dx, ok = pairs[group - 1]

            def push_all(group=group, dx=dx, far_off=far_off):
                for k in far_off:
                    push(group, dx, k)

            pl.when(ok)(push_all)
        for k in far_off:
            if k:
                push(0, 0, k)
    kept = pltpu.make_async_copy(rs, rr.at[pl.ds(place, 1)], gather_sem.at[3])
    kept.start()

    def gathered(sem, first, size):
        some = rr.at[pl.ds(first, size)]
        pltpu.make_async_copy(some, some, gather_sem.at[sem]).wait()

    after = plain - column_terms(smooth, dsmooth)
    for dx, part in zip((-1, 0, 1), parts):
        after = after + turn(part, -dx, 1)
    rest = line_solve([after[layer] for layer in range(LAYERS)], *own_factors)
    for layer in range(LAYERS):
        ans[layer] = smooth[layer] + rest[layer]
    for d, (dx, _) in enumerate(OFFSETS):
        ws[:, d] = turn(cs[d], -dx, 1)
    for layer, held in enumerate(line_solve([ws[i] for i in range(LAYERS)], *own_factors)):
        ws[layer] = held

    received(coarse)
    operators = []
    for f, c in ((cf, cc), (cf_near.at[0], cc_near.at[0]), (cf_near.at[1], cc_near.at[1])):
        scale = OMEGA / f[0]
        cols = [c[k] for k in range(4)]
        weights = [f[1 + k] * scale for k in range(4)]
        operators.append((scale, weights, [a >> 7 for a in cols], [a & 127 for a in cols]))
    agg_all = jnp.where(core, own[AGG], near[AGG])
    agg_all = jnp.where(row_ok, agg_all, 0.0).astype(I32)
    sent(round1 + coarse)
    low = lax.broadcasted_iota(I32, (n_hi, 128), 1) < AGG_DEV

    def picked(source, at):
        return jnp.take_along_axis(source, at, axis=1, mode="promise_in_bounds")

    for g, (scale, weights, col_hi, col_lo) in enumerate(operators):
        if g == 0:
            gathered(3, 0, n_py)
        else:
            pl.when(pairs[g - 1][1])(functools.partial(gathered, 3 + g, g * n_py, n_py))
        evens = rr[g * n_py : g * n_py + n_hi, 0, :]
        odds = rr[g * n_py + n_hi : (g + 1) * n_py, 0, :]
        target = [
            jnp.where(low, evens, turn(odds, AGG_DEV, 1)) * scale,
            jnp.where(low, turn(evens, AGG_DEV, 1), odds) * scale,
        ]
        iterate = target
        for _ in range(CITERS - 1):
            later = []
            for c in range(2):
                rows = [
                    jnp.broadcast_to(iterate[c][h : h + 1], (n_hi, 128)) for h in range(n_hi)
                ]
                value = (1.0 - OMEGA) * iterate[c] + target[c]
                for k in range(4):
                    found = picked(rows[0], col_lo[k])
                    for h in range(1, n_hi):
                        found = jnp.where(col_hi[k] == h, picked(rows[h], col_lo[k]), found)
                    value = value - weights[k] * found
                later.append(value)
            iterate = later
        xs[g, 0] = iterate[0]
        xs[g, 1] = iterate[1]

    def corrected(owner, at):
        h = pl.ds(lax.div(owner, 2), 1)
        below, here, above = (
            jnp.where(sub < 4, xs[g, 0, h, :], xs[g, 1, h, :]) for g in (2 - odd, 0, 1 + odd)
        )
        source = jnp.where(row == 0, below, jnp.where(row == 3, above, here))
        return picked(source, at + AGG_DEV * lax.rem(owner, 2))

    edge_agg = edge0.astype(I32)
    agg_left = jnp.broadcast_to(edge_agg[:, 42:43], (8, 128))
    agg_right = jnp.broadcast_to(edge_agg[:, 41:42], (8, 128))
    corr = jnp.where(row_ok, corrected(py, agg_all), 0.0)
    corr_edge = jnp.where(
        half == 0,
        corrected(wrap(py - 1, n_py), agg_left),
        corrected(wrap(py + 1, n_py), agg_right),
    )
    corr_edge = jnp.where(row_ok & half_ok, corr_edge, 0.0)
    corr_beside = beside(corr, corr_edge)
    result = ans[...]
    for d, (dx, dy) in enumerate(OFFSETS):
        result = result + ws[:, d] * turn(corr_beside[dy + 1], -dx, 0)
    ans[...] = result
    gathered(0, 0, n_py - 1)
    for group, (_, ok) in enumerate(pairs):
        pl.when(ok)(functools.partial(gathered, 1 + group, 0, n_py))


def write_out(image, answer, image_out, answer_out, sems):
    copies = []
    for c in range(2):
        rows = pl.ds(4 * c + 1, 2)
        copies.append(pltpu.make_async_copy(image.at[:, rows], image_out.at[c], sems.at[c]))
        copies.append(pltpu.make_async_copy(answer.at[:, rows], answer_out.at[c], sems.at[2 + c]))
    for copy in copies:
        copy.start()
    for copy in copies:
        copy.wait()


def solution(mesh):
    n_px, n_py = mesh.shape["px"], mesh.shape["py"]
    n_hi = n_py // 2
    n_sends = 18

    def body(
        velocity, direction, forcing, softness, friction, links, aggregate, diag, vals, cols
    ):
        block = jax.ShapeDtypeStruct(velocity.shape, F32)
        wide = jax.ShapeDtypeStruct((LAYERS, 8, 128), F32)
        results = pl.pallas_call(
            functools.partial(kernel, n_px, n_py),
            out_shape=(wide, wide),
            in_specs=[pl.BlockSpec(memory_space=pltpu.HBM)] * 10,
            out_specs=[pl.BlockSpec(memory_space=pltpu.VMEM)] * 2,
            scratch_shapes=[
                pltpu.VMEM((PLANES, 8, 128), F32),
                pltpu.VMEM((PLANES, 8, 128), F32),
                pltpu.VMEM((FAR, 8, 128), F32),
                pltpu.VMEM((4, 8, 128), I32),
                pltpu.VMEM((8, 128), I32),
                pltpu.VMEM((5, n_hi, 128), F32),
                pltpu.VMEM((4, n_hi, 128), I32),
                pltpu.VMEM((2, 5, n_hi, 128), F32),
                pltpu.VMEM((2, 4, n_hi, 128), I32),
                pltpu.VMEM((3, 8, 128), F32),
                pltpu.VMEM((6, 3, 8, 128), F32),
                pltpu.VMEM((1, 1, 128), F32),
                pltpu.VMEM((3 * n_py, 1, 128), F32),
                pltpu.VMEM((3, 2, n_hi, 128), F32),
                pltpu.VMEM((8, LAYERS, 8, 128), F32),
                pltpu.VMEM((8, LAYERS, 8, 128), F32),
                pltpu.VMEM((LAYERS, 8, 8, 128), F32),
                pltpu.SemaphoreType.DMA((23,)),
                pltpu.SemaphoreType.DMA((n_sends,)),
                pltpu.SemaphoreType.DMA((n_sends,)),
                pltpu.SemaphoreType.DMA((6,)),
                pltpu.SemaphoreType.REGULAR,
                pltpu.SemaphoreType.REGULAR,
            ],
            compiler_params=pltpu.CompilerParams(
                collective_id=0, has_side_effects=True, vmem_limit_bytes=32 * 1024 * 1024
            ),
        )(
            *(
                pltpu.with_memory_space_constraint(a, pltpu.HBM)
                for a in (
                    velocity,
                    direction,
                    forcing,
                    softness,
                    friction,
                    links,
                    aggregate,
                    diag.reshape(n_hi, 128),
                    vals.reshape(4, n_hi, 128).transpose(1, 0, 2),
                    cols.reshape(4, n_hi, 128).transpose(1, 0, 2),
                )
            )
        )
        return pl.pallas_call(
            write_out,
            out_shape=(block, block),
            in_specs=[pl.BlockSpec(memory_space=pl.ANY)] * 2,
            out_specs=[pl.BlockSpec(memory_space=pltpu.HBM)] * 2,
            scratch_shapes=[pltpu.SemaphoreType.DMA((4,))],
            compiler_params=pltpu.CompilerParams(vmem_limit_bytes=8 * 1024 * 1024),
        )(*results)

    return jax.shard_map(
        body,
        mesh=mesh,
        in_specs=(
            P(None, None, "px", "py"),
            P(None, None, "px", "py"),
            P(None, None, "px", "py"),
            P("px", "py"),
            P("px", "py"),
            P(None, "px", "py"),
            P("px", "py"),
            P("px"),
            P(None, "px"),
            P(None, "px"),
        ),
        out_specs=(P(None, None, "px", "py"), P(None, None, "px", "py")),
        check_vma=False,
    )
```

```python
import functools

import jax
import jax.numpy as jnp
from jax import lax
from jax.experimental import pallas as pl
from jax.experimental.pallas import tpu as pltpu
from jax.sharding import PartitionSpec as P

CITERS = 4
AGG_DEV = 64
KZ = 4.0
EPS0 = 0.05
OMEGA = 0.8
OFFSETS = ((-1, -1), (-1, 0), (-1, 1), (0, -1), (0, 1), (1, -1), (1, 0), (1, 1))
MESH = pl.DeviceIdType.MESH
LAYERS = 20
F32 = jnp.float32
I32 = jnp.int32

FIELD = 64
REACH = 4
V, X, RATE, LOAD, RUB, SLOT, AGG = 0, LAYERS, 2 * LAYERS, 2 * LAYERS + 1, 61, 62, 66
FAR, PLANES = 2 * LAYERS + 1, 67


def turn(x, shift, axis):
    shift %= x.shape[axis]
    return pltpu.roll(x, shift, axis) if shift else x


def stacked(tiles):
    return jnp.concatenate([t[None] for t in tiles], axis=0)


def vertical(x):
    return jnp.concatenate([x[1:], x[-1:]], axis=0) - jnp.concatenate([x[:1], x[:-1]], axis=0)


def kernel(
    n_px,
    n_py,
    velocity,
    direction,
    forcing,
    softness,
    friction,
    links,
    aggregate,
    coarse_diag,
    coarse_vals,
    coarse_cols,
    img,
    ans,
    own,
    near,
    far,
    lk,
    ag,
    cf,
    cc,
    cf_near,
    cc_near,
    edge_send,
    edge_recv,
    rs,
    rr,
    xs,
    cs,
    ds_,
    ws,
    load_sem,
    send_sem,
    recv_sem,
    gather_sem,
    relay,
    complete,
):
    px = lax.axis_index("px")
    py = lax.axis_index("py")
    n_hi = n_py // 2

    def wrap(value, count):
        return lax.rem(value + count, count)

    def peer(dx, dy):
        return (wrap(px + dx, n_px), wrap(py + dy, n_py))

    def inside_grid(dx, dy):
        ok = (px >= 0) if dx == 0 else (px > 0) if dx < 0 else (px < n_px - 1)
        return ok if dy == 0 else ok & ((py > 0) if dy < 0 else (py < n_py - 1))

    barrier = pltpu.get_barrier_semaphore()

    def greet(dx, dy):
        pl.semaphore_signal(barrier, inc=1, device_id=peer(dx, dy), device_id_type=MESH)

    line = [k for k in range(1, n_py) if min(k, n_py - k) <= REACH]
    line.sort(key=lambda k: -min(k, n_py - k))
    expected = len(line)
    for k in line[:2]:
        greet(0, k)
    for dx in (-1, 1):
        for dy in (-1, 1, 0):
            pl.when(inside_grid(dx, dy))(functools.partial(greet, dx, dy))
            expected = expected + jnp.where(inside_grid(dx, dy), 1, 0)
    for k in line[2:]:
        greet(0, k)
    relayed = n_py // 2 > REACH

    loads = []

    def load(src, dst):
        copy = pltpu.make_async_copy(src, dst, load_sem.at[len(loads)])
        copy.start()
        loads.append(copy)

    for c in range(2):
        rows = pl.ds(4 * c + 1, 2)
        load(velocity.at[c], own.at[pl.ds(V, LAYERS), rows])
        load(direction.at[c], own.at[pl.ds(X, LAYERS), rows])
        load(softness, own.at[RATE, rows])
        load(forcing.at[c], own.at[pl.ds(LOAD, LAYERS), rows])
        load(friction, own.at[RUB, rows])
        load(links, lk.at[:, rows])
        load(aggregate, ag.at[rows])
    first_loads = len(loads)
    load(coarse_diag, cf.at[0])
    for k in range(4):
        load(coarse_vals.at[:, k], cf.at[1 + k])
        load(coarse_cols.at[:, k], cc.at[k])

    lane = lax.broadcasted_iota(I32, (8, 128), 1)
    sub = lax.broadcasted_iota(I32, (8, 128), 0)
    row = sub & 3
    core = (row == 1) | (row == 2)
    none = 9
    no_below = jnp.where(px > 0, none, 0)
    no_above = jnp.where(px < n_px - 1, none, 3)
    row_ok = (row != no_below) & (row != no_above)
    far_ok = row_ok & ((row == 0) | (row == 3))
    even = (lane & 1) == 0
    no_left = jnp.where(py > 0, none, 0)
    no_right = jnp.where(py < n_py - 1, none, 1)
    side_ok = ((lane & 1) != no_left) & ((lane & 1) != no_right)
    half = lane >> 6
    half_ok = (half != no_left) & (half != no_right)

    count = [0]

    def send(src, dst, target, to_ok, from_ok):
        i = count[0]
        count[0] += 1
        copy = pltpu.make_async_remote_copy(
            src_ref=src,
            dst_ref=dst,
            send_sem=send_sem.at[i],
            recv_sem=recv_sem.at[i],
            device_id=target,
            device_id_type=MESH,
        )
        pl.when(to_ok)(copy.start)
        return copy, to_ok, from_ok

    def received(copies):
        for copy, _, from_ok in copies:
            pl.when(from_ok)(copy.wait_recv)

    def sent(copies):
        for copy, to_ok, _ in copies:
            pl.when(to_ok)(copy.wait_send)

    def packed(fields, shift, gap):
        tile = jnp.zeros((8, 128), F32)
        for x, at in fields:
            put = (lane == at % 128) | (lane == (at + gap) % 128)
            tile = jnp.where(put, turn(x, at + shift, 1), tile)
        return tile

    def unpacked(tile):
        return stacked([turn(tile, -(FIELD + 2 * layer), 1) for layer in range(LAYERS)])

    def beside(x, ends):
        left = jnp.where(lane == 0, ends, turn(x, 1, x.ndim - 1))
        right = jnp.where(lane == 127, ends, turn(x, -1, x.ndim - 1))
        return left, x, right

    for copy in loads[:first_loads]:
        copy.wait()
    agg_own = jnp.where(core, ag[...], 0)
    own[AGG] = agg_own.astype(F32)
    for k in range(4):
        own[SLOT + k] = jnp.where(core, lk[k], 8).astype(F32)
    moving = [(own[V + i], 2 * i) for i in range(LAYERS)]
    moving += [(own[X + i], FIELD + 2 * i) for i in range(LAYERS)]
    moving += [(own[RATE], 2 * LAYERS)]
    fixed = [(own[AGG], 42), (own[RUB], 44)] + [(own[SLOT + k], 46 + 2 * k) for k in range(4)]
    edge_send[0] = packed(moving + fixed, 1, 1)
    edge_send[1] = packed(moving, 2, 3)
    edge_send[2] = packed([(own[LOAD + i], FIELD + 2 * i) for i in range(LAYERS)], 1, 1)
    pl.semaphore_wait(barrier, expected)
    if relayed:
        for k in (REACH, n_py - REACH):
            pl.semaphore_signal(relay, inc=1, device_id=peer(0, k), device_id_type=MESH)
    slot = {(dx, dy): 3 * (dy > 0) + dx + 1 for dx in (-1, 0, 1) for dy in (-1, 1)}
    round1 = []
    def send_round1(src, dst, dx, dy):
        to_ok, from_ok = inside_grid(dx, dy), inside_grid(-dx, -dy)
        round1.append(send(src, dst, peer(dx, dy), to_ok, from_ok))

    for dx in (-1, 1):
        for dy in (-1, 1):
            send_round1(edge_send, edge_recv.at[slot[-dx, -dy]], dx, dy)
    for c in range(2):
        low, high = 4 * c + 1, 4 * c + 2
        for dx, first, second, to in ((1, high, low, 4 * c), (-1, low, high, 4 * c + 3)):
            there = pl.ds(to, 1)
            send_round1(own.at[:, pl.ds(first, 1)], near.at[:, there], dx, 0)
            moved = own.at[pl.ds(0, FAR), pl.ds(second, 1)]
            send_round1(moved, far.at[:, there], dx, 0)
    for dy in (-1, 1):
        send_round1(edge_send, edge_recv.at[slot[0, -dy]], 0, dy)

    odd = lax.rem(px, 2)
    pairs = []
    for dx in (1 - 2 * odd, 2 * odd - 1):
        pairs.append((dx, (px + dx >= 0) & (px + dx < n_px)))
    for copy in loads[first_loads:]:
        copy.wait()
    coarse = []
    for i, (dx, ok) in enumerate(pairs):
        coarse.append(send(cf, cf_near.at[i], peer(dx, 0), ok, ok))
        coarse.append(send(cc, cc_near.at[i], peer(dx, 0), ok, ok))
    if relayed:
        pl.semaphore_wait(relay, 2)
    lines = 0
    for dx in (-1, 1):

        def tell(dx=dx):
            pl.semaphore_signal(complete, inc=1, device_id=peer(dx, 0), device_id_type=MESH)

        pl.when(inside_grid(dx, 0))(tell)
        lines = lines + jnp.where(inside_grid(dx, 0), 1, 0)
    agg_rows = [agg_own[r : r + 1, :] for r in (1, 2)]
    ids = lax.broadcasted_iota(I32, (128, 128), 0) & (AGG_DEV - 1)
    hot = [(ids == a).astype(F32) for a in agg_rows]

    tiles = round1[:4] + round1[-2:]
    received(tiles)

    def joined(first, size):
        here = jnp.where(core, own[first : first + size], near[first : first + size])
        return jnp.where(row_ok, here, 0.0)

    def outer(first, size):
        return jnp.where(far_ok, far[first : first + size], 0.0)

    def edges(i):
        shift = -4 if i == 1 else -2

        def both(column):
            left, right = column(0), column(3)
            return jnp.where(side_ok, jnp.where(even, left, turn(right, shift, 1)), 0.0)

        def inner_rows(first):
            below, here, above = (edge_recv[first + j, i] for j in range(3))
            return jnp.where(
                row == 0, turn(below, -2, 0), jnp.where(row == 3, turn(above, 2, 0), here)
            )

        def outer_rows(first):
            below, above = edge_recv[first, i], edge_recv[first + 2, i]
            return jnp.where(row == 0, turn(below, -1, 0), turn(above, 1, 0))

        return (
            jnp.where(row_ok, both(inner_rows), 0.0),
            jnp.where(far_ok, both(outer_rows), 0.0) if i < 2 else None,
        )

    top = (lane == 38) | (lane == 37) | (lane == 102) | (lane == 101)
    bottom = (lane == 0) | (lane == 127) | (lane == 64) | (lane == 63)

    def edge_vertical(tile):
        return jnp.where(top, tile, turn(tile, -2, 1)) - jnp.where(bottom, tile, turn(tile, 2, 1))

    def viscosity(shear, soft):
        axis = shear.ndim - 2
        square = shear * shear
        strain = EPS0 + 0.25 * KZ * (square + turn(square, 4, axis))
        log = jnp.log(strain)
        eta = soft * jnp.exp(log * (-1.0 / 3.0))
        slope = (-2.0 / 3.0 * 0.25 * KZ) * soft * jnp.exp(log * (-4.0 / 3.0)) * shear
        return eta, slope

    def derived(slope, shear):
        rise = slope * shear
        return rise + turn(rise, 4, rise.ndim - 2)

    def state(v, x, rate):
        eta, slope = viscosity(vertical(v), rate)
        return (eta, v, x, derived(slope, vertical(x))), slope

    def edge_state(tile):
        shear = edge_vertical(tile)
        eta, slope = viscosity(shear, jnp.where(even, tile[:, 40:41], tile[:, 39:40]))
        slope = turn(slope, FIELD, 1)
        return (turn(eta, FIELD, 1), turn(tile, FIELD, 1), tile, derived(slope, shear)), slope

    def inside(v, x, rate):
        fields = [(v[i], 2 * i) for i in range(LAYERS)]
        fields += [(x[i], FIELD + 2 * i) for i in range(LAYERS)] + [(rate[0], 2 * LAYERS)]
        return packed(fields, 0, -1)

    edge0, rim_edge0 = edges(0)
    edge1, rim_edge1 = edges(1)
    edge_load, _ = edges(2)
    at_edge, edge_slope = edge_state(edge0)
    rim_at_edge, _ = edge_state(rim_edge0)
    past_edge, _ = edge_state(edge1)
    rim_past_edge, _ = edge_state(rim_edge1)
    ends_at = [unpacked(e) for e in at_edge]
    rim_ends_at = [unpacked(e) for e in rim_at_edge]

    received(round1[4:-2])
    halo = (joined(V, LAYERS), joined(X, LAYERS), joined(RATE, 1))
    rim = (outer(V, LAYERS), outer(X, LAYERS), outer(RATE, 1))
    here, slope = state(*halo)
    rim_here, _ = state(*rim)
    in_edge, _ = edge_state(inside(*halo))
    rim_in_edge, _ = edge_state(inside(*rim))

    def triples(states, ends):
        found = [beside(a, e) for a, e in zip(states, ends)]
        return [tuple(f[i] for f in found) for i in range(3)]

    def edge_triples(past, at, within):
        left = tuple(jnp.where(even, a, b) for a, b in zip(past, within))
        right = tuple(jnp.where(even, b, a) for a, b in zip(past, within))
        return [left, at, right]

    def halves_of(slots):
        found = []
        for d in range(len(OFFSETS)):
            tally = (slots[0] == d).astype(F32)
            for other in slots[1:]:
                tally = tally + (other == d).astype(F32)
            found.append(0.5 * tally)
        return found

    def coupling(halves, centre, around, beyond, keep):
        eta, v = centre[:2]
        axis = eta.ndim - 2
        side = pull = part = 0.0
        for dx in (-1, 0, 1):
            eta_here, v_here = turn(eta, dx, axis), turn(v, dx, axis)
            sums = [0.0, 0.0, 0.0]
            for d, (ox, oy) in enumerate(OFFSETS):
                if ox != dx:
                    continue
                weight = turn(halves[d], dx, 0)
                if dx != 0:
                    weight = jnp.where(row == (3 if dx < 0 else 0), 0.0, weight)
                eta_n, v_n, x_n, deta_n = around[oy + 1]
                couple = weight * (eta_here + eta_n)
                drop = weight * (v_here - v_n)
                if keep:
                    cs[d] = couple
                    ds_[d] = drop
                sums = [sums[0] + couple, sums[1] + drop, sums[2] + (drop * deta_n - couple * x_n)]
            side, pull, part = (
                old + turn(new, -dx, axis) for old, new in zip((side, pull, part), sums)
            )
        for oy in (-1, 0, 1):
            weight = jnp.where(row == 0, halves[OFFSETS.index((-1, oy))], 0.0)
            weight = jnp.where(row == 3, halves[OFFSETS.index((1, oy))], weight)
            eta_n, v_n, x_n, deta_n = beyond[oy + 1]
            couple = weight * (eta + eta_n)
            drop = weight * (v - v_n)
            side, pull = side + couple, pull + drop
            part = part + (drop * deta_n - couple * x_n)
        return side, pull, part

    eta, v, x, deta = here
    links_here = jnp.where(core, own[SLOT : SLOT + 4], near[SLOT : SLOT + 4])
    rub = jnp.where(core, own[RUB], near[RUB])
    side, pull, part = coupling(
        halves_of([links_here[k] for k in range(4)]),
        here,
        triples(here, ends_at),
        triples(rim_here, rim_ends_at),
        True,
    )
    face = (0.5 * KZ) * (eta[:-1] + eta[1:])
    jump = (0.5 * KZ) * (v[1:] - v[:-1])

    def column_terms(x, deta):
        flux = face * (x[1:] - x[:-1]) + jump * (deta[1:] + deta[:-1])
        return jnp.concatenate([rub * x[:1] - flux[:1], flux[:-1] - flux[1:], flux[-1:]])

    image = side * x + pull * deta + part + column_terms(x, deta)
    img[...] = image
    resid = joined(LOAD, LAYERS) - image

    def of_edge(at):
        return jnp.where(even, edge0[:, at : at + 1], edge0[:, at - 1 : at])

    edge_side, edge_pull, edge_part = coupling(
        halves_of([of_edge(46 + 2 * k) for k in range(4)]),
        at_edge,
        edge_triples(past_edge, at_edge, in_edge),
        edge_triples(rim_past_edge, rim_at_edge, rim_in_edge),
        False,
    )
    eta_e, v_e, x_e, deta_e = at_edge
    edge_rub = of_edge(44)

    def upper_of(tile):
        return turn(tile, -2, 1)

    edge_face = jnp.where(top, 0.0, (0.5 * KZ) * (eta_e + upper_of(eta_e)))
    edge_jump = (0.5 * KZ) * (upper_of(v_e) - v_e)
    flux = edge_face * (upper_of(x_e) - x_e) + edge_jump * (upper_of(deta_e) + deta_e)
    flux = jnp.where(top, 0.0, flux)
    edge_image = edge_side * x_e + edge_pull * deta_e + edge_part - flux
    edge_image = edge_image + jnp.where(bottom, edge_rub * x_e, turn(flux, 2, 1))
    edge_resid = unpacked(edge_load - edge_image)

    side2 = [stacked(pair) for pair in zip(side, unpacked(edge_side))]
    face2 = [stacked(pair) for pair in zip(face, unpacked(edge_face))]
    ends_rub = jnp.where(lane < 64, edge0[:, 44:45], edge0[:, 43:44])
    middle = LAYERS // 2
    inverse2, inward2, outward2 = [None] * LAYERS, [None] * LAYERS, [None] * LAYERS

    def eliminate(layer, before, after):
        pivot = side2[layer]
        if layer == 0:
            pivot = pivot + stacked([rub, ends_rub])
        if after is not None:
            pivot = pivot + face2[after]
        if before is not None:
            previous = layer - 1 if layer < middle else layer + 1
            pivot = pivot + face2[before] - face2[before] * outward2[previous]
        inv = 1.0 / pivot
        inverse2[layer] = inv
        inward2[layer] = None if before is None else face2[before] * inv
        outward2[layer] = None if after is None else face2[after] * inv

    for step in range(middle):
        eliminate(step, step - 1 if step else None, step)
        layer = LAYERS - 1 - step
        eliminate(layer, layer if step else None, layer - 1)
    meet2 = 1.0 / (1.0 - outward2[middle - 1] * outward2[middle])

    def line_solve(rhs, inverse, inward, outward, meet):
        found = [None] * LAYERS
        for step in range(middle):
            for layer, previous in ((step, step - 1), (LAYERS - 1 - step, LAYERS - step)):
                found[layer] = rhs[layer] * inverse[layer]
                if step:
                    found[layer] = found[layer] + inward[layer] * found[previous]
        low, high = middle - 1, middle
        found[low] = (found[low] + outward[low] * found[high]) * meet
        found[high] = found[high] + outward[high] * found[low]
        for step in range(1, middle):
            for layer, previous in ((low - step, low - step + 1), (high + step, high + step - 1)):
                found[layer] = found[layer] + outward[layer] * found[previous]
        return found

    solved = line_solve(
        [stacked(p) for p in zip(resid, edge_resid)], inverse2, inward2, outward2, meet2
    )
    own_factors = [
        [a if a is None else a[0] for a in factor] for factor in (inverse2, inward2, outward2)
    ] + [meet2[0]]
    smooth = jnp.where(row_ok, stacked([a[0] for a in solved]), 0.0)
    ends = jnp.where(row_ok & half_ok, stacked([a[1] for a in solved]), 0.0)

    dsmooth = derived(slope, vertical(smooth))
    dends = derived(unpacked(edge_slope), vertical(ends))
    smooth_beside = beside(smooth, ends)
    dsmooth_beside = beside(dsmooth, dends)
    plain = resid - (side * smooth + pull * dsmooth)
    parts = []
    for dx in (-1, 0, 1):
        part = 0.0
        for d, (ox, oy) in enumerate(OFFSETS):
            if ox == dx:
                part = part + (cs[d] * smooth_beside[oy + 1] - ds_[d] * dsmooth_beside[oy + 1])
        parts.append(part)
    total = jnp.sum(plain, axis=0) - rub * smooth[0]
    for dx, part in zip((-1, 0, 1), parts):
        total = total + turn(jnp.sum(part, axis=0), -dx, 0)
    mean = jnp.where(core, total / LAYERS, 0.0)

    pieces, rest_of = [], mean
    for _ in range(2):
        large = rest_of * 65537.0
        piece = large - (large - rest_of)
        pieces.append(piece)
        rest_of = rest_of - piece
    pieces.append(rest_of)
    pieces = jnp.concatenate(pieces, axis=0)
    sums = lax.dot_general(
        jnp.concatenate([pieces, turn(pieces, -1, 0)], axis=1),
        jnp.concatenate(hot, axis=1),
        (((1,), (1,)), ((), ())),
        preferred_element_type=F32,
    )
    sums = sums[0:8] + sums[8:16] + sums[16:24]
    mine = jnp.where(lane[0:1] < AGG_DEV, sums[1:2], sums[5:6])
    rs[0] = mine
    place = lax.rem(py, 2) * n_hi + lax.div(py, 2)

    def push(group, dx, k):
        pltpu.make_async_remote_copy(
            src_ref=rs,
            dst_ref=rr.at[pl.ds(group * n_py + place, 1)],
            send_sem=gather_sem.at[group],
            recv_sem=gather_sem.at[3 + group],
            device_id=peer(dx, k),
            device_id_type=MESH,
        ).start()

    pl.semaphore_wait(complete, lines)
    for reach in range(n_py // 2, -1, -1):
        far_off = sorted({reach, (n_py - reach) % n_py})
        for group in (2, 1):
            dx, ok = pairs[group - 1]

            def push_all(group=group, dx=dx, far_off=far_off):
                for k in far_off:
                    push(group, dx, k)

            pl.when(ok)(push_all)
        for k in far_off:
            if k:
                push(0, 0, k)
    kept = pltpu.make_async_copy(rs, rr.at[pl.ds(place, 1)], gather_sem.at[3])
    kept.start()

    def gathered(sem, first, size):
        some = rr.at[pl.ds(first, size)]
        pltpu.make_async_copy(some, some, gather_sem.at[sem]).wait()

    after = plain - column_terms(smooth, dsmooth)
    for dx, part in zip((-1, 0, 1), parts):
        after = after + turn(part, -dx, 1)
    rest = line_solve([after[layer] for layer in range(LAYERS)], *own_factors)
    for layer in range(LAYERS):
        ans[layer] = smooth[layer] + rest[layer]
    for d, (dx, _) in enumerate(OFFSETS):
        ws[:, d] = turn(cs[d], -dx, 1)
    for layer, held in enumerate(line_solve([ws[i] for i in range(LAYERS)], *own_factors)):
        ws[layer] = held

    received(coarse)
    operators = []
    for f, c in ((cf, cc), (cf_near.at[0], cc_near.at[0]), (cf_near.at[1], cc_near.at[1])):
        scale = OMEGA / f[0]
        cols = [c[k] for k in range(4)]
        weights = [f[1 + k] * scale for k in range(4)]
        bits = [
            [((a >> (7 + b)) & 1) == 1 for b in range((n_hi - 1).bit_length())] for a in cols
        ]
        operators.append((scale, weights, bits, [a & 127 for a in cols]))
    agg_all = jnp.where(core, own[AGG], near[AGG])
    agg_all = jnp.where(row_ok, agg_all, 0.0).astype(I32)
    sent(round1 + coarse)
    gathered(0, 0, n_py - 1)
    for group, (_, ok) in enumerate(pairs):
        pl.when(ok)(functools.partial(gathered, 1 + group, 0, n_py))
    low = lax.broadcasted_iota(I32, (n_hi, 128), 1) < AGG_DEV

    def picked(source, at):
        return jnp.take_along_axis(source, at, axis=1, mode="promise_in_bounds")

    for g, (scale, weights, col_bits, col_lo) in enumerate(operators):
        if g == 0:
            gathered(3, 0, n_py)
        else:
            pl.when(pairs[g - 1][1])(functools.partial(gathered, 3 + g, g * n_py, n_py))
        evens = rr[g * n_py : g * n_py + n_hi, 0, :]
        odds = rr[g * n_py + n_hi : (g + 1) * n_py, 0, :]
        target = [
            jnp.where(low, evens, turn(odds, AGG_DEV, 1)) * scale,
            jnp.where(low, turn(evens, AGG_DEV, 1), odds) * scale,
        ]
        iterate = target
        for _ in range(CITERS - 1):
            later = []
            for c in range(2):
                rows = [
                    jnp.broadcast_to(iterate[c][h : h + 1], (n_hi, 128)) for h in range(n_hi)
                ]
                value = (1.0 - OMEGA) * iterate[c] + target[c]
                for k in range(4):
                    found = [picked(r, col_lo[k]) for r in rows]
                    for bit in col_bits[k]:
                        found = [
                            jnp.where(bit, b, a) for a, b in zip(found[::2], found[1::2])
                        ]
                    value = value - weights[k] * found[0]
                later.append(value)
            iterate = later
        xs[g, 0] = iterate[0]
        xs[g, 1] = iterate[1]

    def corrected(owner, at):
        h = pl.ds(lax.div(owner, 2), 1)
        below, here, above = (
            jnp.where(sub < 4, xs[g, 0, h, :], xs[g, 1, h, :]) for g in (2 - odd, 0, 1 + odd)
        )
        source = jnp.where(row == 0, below, jnp.where(row == 3, above, here))
        return picked(source, at + AGG_DEV * lax.rem(owner, 2))

    edge_agg = edge0.astype(I32)
    agg_left = jnp.broadcast_to(edge_agg[:, 42:43], (8, 128))
    agg_right = jnp.broadcast_to(edge_agg[:, 41:42], (8, 128))
    corr = jnp.where(row_ok, corrected(py, agg_all), 0.0)
    corr_edge = jnp.where(
        half == 0,
        corrected(wrap(py - 1, n_py), agg_left),
        corrected(wrap(py + 1, n_py), agg_right),
    )
    corr_edge = jnp.where(row_ok & half_ok, corr_edge, 0.0)
    corr_beside = beside(corr, corr_edge)
    result = ans[...]
    for d, (dx, dy) in enumerate(OFFSETS):
        result = result + ws[:, d] * turn(corr_beside[dy + 1], -dx, 0)
    ans[...] = result


def write_out(image, answer, image_out, answer_out, sems):
    copies = []
    for c in range(2):
        rows = pl.ds(4 * c + 1, 2)
        copies.append(pltpu.make_async_copy(image.at[:, rows], image_out.at[c], sems.at[c]))
        copies.append(pltpu.make_async_copy(answer.at[:, rows], answer_out.at[c], sems.at[2 + c]))
    for copy in copies:
        copy.start()
    for copy in copies:
        copy.wait()


def solution(mesh):
    n_px, n_py = mesh.shape["px"], mesh.shape["py"]
    n_hi = n_py // 2
    n_sends = 18

    def body(
        velocity, direction, forcing, softness, friction, links, aggregate, diag, vals, cols
    ):
        block = jax.ShapeDtypeStruct(velocity.shape, F32)
        wide = jax.ShapeDtypeStruct((LAYERS, 8, 128), F32)
        results = pl.pallas_call(
            functools.partial(kernel, n_px, n_py),
            out_shape=(wide, wide),
            in_specs=[pl.BlockSpec(memory_space=pltpu.HBM)] * 10,
            out_specs=[pl.BlockSpec(memory_space=pltpu.VMEM)] * 2,
            scratch_shapes=[
                pltpu.VMEM((PLANES, 8, 128), F32),
                pltpu.VMEM((PLANES, 8, 128), F32),
                pltpu.VMEM((FAR, 8, 128), F32),
                pltpu.VMEM((4, 8, 128), I32),
                pltpu.VMEM((8, 128), I32),
                pltpu.VMEM((5, n_hi, 128), F32),
                pltpu.VMEM((4, n_hi, 128), I32),
                pltpu.VMEM((2, 5, n_hi, 128), F32),
                pltpu.VMEM((2, 4, n_hi, 128), I32),
                pltpu.VMEM((3, 8, 128), F32),
                pltpu.VMEM((6, 3, 8, 128), F32),
                pltpu.VMEM((1, 1, 128), F32),
                pltpu.VMEM((3 * n_py, 1, 128), F32),
                pltpu.VMEM((3, 2, n_hi, 128), F32),
                pltpu.VMEM((8, LAYERS, 8, 128), F32),
                pltpu.VMEM((8, LAYERS, 8, 128), F32),
                pltpu.VMEM((LAYERS, 8, 8, 128), F32),
                pltpu.SemaphoreType.DMA((23,)),
                pltpu.SemaphoreType.DMA((n_sends,)),
                pltpu.SemaphoreType.DMA((n_sends,)),
                pltpu.SemaphoreType.DMA((6,)),
                pltpu.SemaphoreType.REGULAR,
                pltpu.SemaphoreType.REGULAR,
            ],
            compiler_params=pltpu.CompilerParams(
                collective_id=0, has_side_effects=True, vmem_limit_bytes=32 * 1024 * 1024
            ),
        )(
            *(
                pltpu.with_memory_space_constraint(a, pltpu.HBM)
                for a in (
                    velocity,
                    direction,
                    forcing,
                    softness,
                    friction,
                    links,
                    aggregate,
                    diag.reshape(n_hi, 128),
                    vals.reshape(4, n_hi, 128).transpose(1, 0, 2),
                    cols.reshape(4, n_hi, 128).transpose(1, 0, 2),
                )
            )
        )
        return pl.pallas_call(
            write_out,
            out_shape=(block, block),
            in_specs=[pl.BlockSpec(memory_space=pl.ANY)] * 2,
            out_specs=[pl.BlockSpec(memory_space=pltpu.HBM)] * 2,
            scratch_shapes=[pltpu.SemaphoreType.DMA((4,))],
            compiler_params=pltpu.CompilerParams(vmem_limit_bytes=8 * 1024 * 1024),
        )(*results)

    return jax.shard_map(
        body,
        mesh=mesh,
        in_specs=(
            P(None, None, "px", "py"),
            P(None, None, "px", "py"),
            P(None, None, "px", "py"),
            P("px", "py"),
            P("px", "py"),
            P(None, "px", "py"),
            P("px", "py"),
            P("px"),
            P(None, "px"),
            P(None, "px"),
        ),
        out_specs=(P(None, None, "px", "py"), P(None, None, "px", "py")),
        check_vma=False,
    )
```

```python
import functools

import jax
import jax.numpy as jnp
from jax import lax
from jax.experimental import pallas as pl
from jax.experimental.pallas import tpu as pltpu
from jax.sharding import PartitionSpec as P

CITERS = 4
AGG_DEV = 64
KZ = 4.0
EPS0 = 0.05
OMEGA = 0.8
OFFSETS = ((-1, -1), (-1, 0), (-1, 1), (0, -1), (0, 1), (1, -1), (1, 0), (1, 1))
MESH = pl.DeviceIdType.MESH
LAYERS = 20
F32 = jnp.float32
I32 = jnp.int32

FIELD = 64
REACH = 4
V, X, RATE, LOAD, RUB, SLOT, AGG = 0, LAYERS, 2 * LAYERS, 2 * LAYERS + 1, 61, 62, 66
FAR, PLANES = 2 * LAYERS + 1, 67


def turn(x, shift, axis):
    shift %= x.shape[axis]
    return pltpu.roll(x, shift, axis) if shift else x


def stacked(tiles):
    return jnp.concatenate([t[None] for t in tiles], axis=0)


def vertical(x):
    return jnp.concatenate([x[1:], x[-1:]], axis=0) - jnp.concatenate([x[:1], x[:-1]], axis=0)


def kernel(
    n_px,
    n_py,
    velocity,
    direction,
    forcing,
    softness,
    friction,
    links,
    aggregate,
    coarse_diag,
    coarse_vals,
    coarse_cols,
    img,
    ans,
    own,
    near,
    far,
    lk,
    ag,
    cf,
    cc,
    cf_near,
    cc_near,
    edge_send,
    edge_recv,
    rs,
    rr,
    xs,
    cs,
    ds_,
    ws,
    load_sem,
    send_sem,
    recv_sem,
    gather_sem,
    relay,
    complete,
):
    px = lax.axis_index("px")
    py = lax.axis_index("py")
    n_hi = n_py // 2

    def wrap(value, count):
        return lax.rem(value + count, count)

    def peer(dx, dy):
        return (wrap(px + dx, n_px), wrap(py + dy, n_py))

    odd = lax.rem(px, 2)
    pairs = []
    for dx in (1 - 2 * odd, 2 * odd - 1):
        pairs.append((dx, (px + dx >= 0) & (px + dx < n_px)))

    def inside_grid(dx, dy):
        ok = (px >= 0) if dx == 0 else (px > 0) if dx < 0 else (px < n_px - 1)
        return ok if dy == 0 else ok & ((py > 0) if dy < 0 else (py < n_py - 1))

    barrier = pltpu.get_barrier_semaphore()

    def greet(dx, dy):
        pl.semaphore_signal(barrier, inc=1, device_id=peer(dx, dy), device_id_type=MESH)

    line = [k for k in range(1, n_py) if min(k, n_py - k) <= REACH]
    line.sort(key=lambda k: -min(k, n_py - k))
    expected = len(line)
    for dx, ok in pairs[::-1]:
        if dx is pairs[0][0]:
            for k in line[:2]:
                greet(0, k)
        for dy in (-1, 1, 0):
            there = ok if dy == 0 else ok & ((py > 0) if dy < 0 else (py < n_py - 1))
            pl.when(there)(functools.partial(greet, dx, dy))
            expected = expected + jnp.where(there, 1, 0)
    for k in line[2:]:
        greet(0, k)
    relayed = n_py // 2 > REACH

    loads = []

    def load(src, dst):
        copy = pltpu.make_async_copy(src, dst, load_sem.at[len(loads)])
        copy.start()
        loads.append(copy)

    for c in range(2):
        rows = pl.ds(4 * c + 1, 2)
        load(velocity.at[c], own.at[pl.ds(V, LAYERS), rows])
        load(direction.at[c], own.at[pl.ds(X, LAYERS), rows])
        load(softness, own.at[RATE, rows])
        load(forcing.at[c], own.at[pl.ds(LOAD, LAYERS), rows])
        load(friction, own.at[RUB, rows])
        load(links, lk.at[:, rows])
        load(aggregate, ag.at[rows])
    first_loads = len(loads)
    load(coarse_diag, cf.at[0])
    for k in range(4):
        load(coarse_vals.at[:, k], cf.at[1 + k])
        load(coarse_cols.at[:, k], cc.at[k])

    lane = lax.broadcasted_iota(I32, (8, 128), 1)
    sub = lax.broadcasted_iota(I32, (8, 128), 0)
    row = sub & 3
    core = (row == 1) | (row == 2)
    none = 9
    no_below = jnp.where(px > 0, none, 0)
    no_above = jnp.where(px < n_px - 1, none, 3)
    row_ok = (row != no_below) & (row != no_above)
    far_ok = row_ok & ((row == 0) | (row == 3))
    even = (lane & 1) == 0
    no_left = jnp.where(py > 0, none, 0)
    no_right = jnp.where(py < n_py - 1, none, 1)
    side_ok = ((lane & 1) != no_left) & ((lane & 1) != no_right)
    half = lane >> 6
    half_ok = (half != no_left) & (half != no_right)

    count = [0]

    def send(src, dst, target, to_ok, from_ok):
        i = count[0]
        count[0] += 1
        copy = pltpu.make_async_remote_copy(
            src_ref=src,
            dst_ref=dst,
            send_sem=send_sem.at[i],
            recv_sem=recv_sem.at[i],
            device_id=target,
            device_id_type=MESH,
        )
        pl.when(to_ok)(copy.start)
        return copy, to_ok, from_ok

    def received(copies):
        for copy, _, from_ok in copies:
            pl.when(from_ok)(copy.wait_recv)

    def sent(copies):
        for copy, to_ok, _ in copies:
            pl.when(to_ok)(copy.wait_send)

    def packed(fields, shift, gap):
        tile = jnp.zeros((8, 128), F32)
        for x, at in fields:
            put = (lane == at % 128) | (lane == (at + gap) % 128)
            tile = jnp.where(put, turn(x, at + shift, 1), tile)
        return tile

    def unpacked(tile):
        return stacked([turn(tile, -(FIELD + 2 * layer), 1) for layer in range(LAYERS)])

    def beside(x, ends):
        left = jnp.where(lane == 0, ends, turn(x, 1, x.ndim - 1))
        right = jnp.where(lane == 127, ends, turn(x, -1, x.ndim - 1))
        return left, x, right

    for copy in loads[:first_loads]:
        copy.wait()
    agg_own = jnp.where(core, ag[...], 0)
    own[AGG] = agg_own.astype(F32)
    for k in range(4):
        own[SLOT + k] = jnp.where(core, lk[k], 8).astype(F32)
    moving = [(own[V + i], 2 * i) for i in range(LAYERS)]
    moving += [(own[X + i], FIELD + 2 * i) for i in range(LAYERS)]
    moving += [(own[RATE], 2 * LAYERS)]
    fixed = [(own[AGG], 42), (own[RUB], 44)] + [(own[SLOT + k], 46 + 2 * k) for k in range(4)]
    edge_send[0] = packed(moving + fixed, 1, 1)
    edge_send[1] = packed(moving, 2, 3)
    edge_send[2] = packed([(own[LOAD + i], FIELD + 2 * i) for i in range(LAYERS)], 1, 1)
    pl.semaphore_wait(barrier, expected)
    round1 = []

    def along(dy):
        return (py >= 0) if dy == 0 else (py > 0) if dy < 0 else (py < n_py - 1)

    for dx, ok in pairs[::-1]:
        for dy in (-1, 1):
            there = edge_recv.at[3 * (dy < 0) + 1 - dx]
            to_ok, from_ok = ok & along(dy), ok & along(-dy)
            round1.append(send(edge_send, there, peer(dx, dy), to_ok, from_ok))
        if relayed and len(round1) == 2:
            for k in (REACH, n_py - REACH):
                pl.semaphore_signal(relay, inc=1, device_id=peer(0, k), device_id_type=MESH)
    for dx, ok in pairs[::-1]:
        up = lax.div(dx + 1, 2)
        for c in range(2):
            there = pl.ds(4 * c + 3 * (1 - up), 1)
            first, second = pl.ds(4 * c + 1 + up, 1), pl.ds(4 * c + 2 - up, 1)
            round1.append(send(own.at[:, first], near.at[:, there], peer(dx, 0), ok, ok))
            moved = own.at[pl.ds(0, FAR), second]
            round1.append(send(moved, far.at[:, there], peer(dx, 0), ok, ok))
    for dy in (-1, 1):
        there = edge_recv.at[3 * (dy < 0) + 1]
        to_ok, from_ok = along(dy), along(-dy)
        round1.append(send(edge_send, there, peer(0, dy), to_ok, from_ok))

    for copy in loads[first_loads:]:
        copy.wait()
    coarse = []
    for i, (dx, ok) in enumerate(pairs):
        coarse.append(send(cf, cf_near.at[i], peer(dx, 0), ok, ok))
        coarse.append(send(cc, cc_near.at[i], peer(dx, 0), ok, ok))
    if relayed:
        pl.semaphore_wait(relay, 2)
    lines = 0
    for dx in (-1, 1):

        def tell(dx=dx):
            pl.semaphore_signal(complete, inc=1, device_id=peer(dx, 0), device_id_type=MESH)

        pl.when(inside_grid(dx, 0))(tell)
        lines = lines + jnp.where(inside_grid(dx, 0), 1, 0)
    agg_rows = [agg_own[r : r + 1, :] for r in (1, 2)]
    ids = lax.broadcasted_iota(I32, (128, 128), 0) & (AGG_DEV - 1)
    hot = [(ids == a).astype(F32) for a in agg_rows]

    tiles = round1[:4] + round1[-2:]
    received(tiles)

    def joined(first, size):
        here = jnp.where(core, own[first : first + size], near[first : first + size])
        return jnp.where(row_ok, here, 0.0)

    def outer(first, size):
        return jnp.where(far_ok, far[first : first + size], 0.0)

    def edges(i):
        shift = -4 if i == 1 else -2

        def both(column):
            left, right = column(0), column(3)
            return jnp.where(side_ok, jnp.where(even, left, turn(right, shift, 1)), 0.0)

        def inner_rows(first):
            below, here, above = (edge_recv[first + j, i] for j in range(3))
            return jnp.where(
                row == 0, turn(below, -2, 0), jnp.where(row == 3, turn(above, 2, 0), here)
            )

        def outer_rows(first):
            below, above = edge_recv[first, i], edge_recv[first + 2, i]
            return jnp.where(row == 0, turn(below, -1, 0), turn(above, 1, 0))

        return (
            jnp.where(row_ok, both(inner_rows), 0.0),
            jnp.where(far_ok, both(outer_rows), 0.0) if i < 2 else None,
        )

    top = (lane == 38) | (lane == 37) | (lane == 102) | (lane == 101)
    bottom = (lane == 0) | (lane == 127) | (lane == 64) | (lane == 63)

    def edge_vertical(tile):
        return jnp.where(top, tile, turn(tile, -2, 1)) - jnp.where(bottom, tile, turn(tile, 2, 1))

    def viscosity(shear, soft):
        axis = shear.ndim - 2
        square = shear * shear
        strain = EPS0 + 0.25 * KZ * (square + turn(square, 4, axis))
        log = jnp.log(strain)
        eta = soft * jnp.exp(log * (-1.0 / 3.0))
        slope = (-2.0 / 3.0 * 0.25 * KZ) * soft * jnp.exp(log * (-4.0 / 3.0)) * shear
        return eta, slope

    def derived(slope, shear):
        rise = slope * shear
        return rise + turn(rise, 4, rise.ndim - 2)

    def state(v, x, rate):
        eta, slope = viscosity(vertical(v), rate)
        return (eta, v, x, derived(slope, vertical(x))), slope

    def edge_state(tile):
        shear = edge_vertical(tile)
        eta, slope = viscosity(shear, jnp.where(even, tile[:, 40:41], tile[:, 39:40]))
        slope = turn(slope, FIELD, 1)
        return (turn(eta, FIELD, 1), turn(tile, FIELD, 1), tile, derived(slope, shear)), slope

    def inside(v, x, rate):
        fields = [(v[i], 2 * i) for i in range(LAYERS)]
        fields += [(x[i], FIELD + 2 * i) for i in range(LAYERS)] + [(rate[0], 2 * LAYERS)]
        return packed(fields, 0, -1)

    edge0, rim_edge0 = edges(0)
    edge1, rim_edge1 = edges(1)
    edge_load, _ = edges(2)
    at_edge, edge_slope = edge_state(edge0)
    rim_at_edge, _ = edge_state(rim_edge0)
    past_edge, _ = edge_state(edge1)
    rim_past_edge, _ = edge_state(rim_edge1)
    ends_at = [unpacked(e) for e in at_edge]
    rim_ends_at = [unpacked(e) for e in rim_at_edge]

    received(round1[4:-2])
    halo = (joined(V, LAYERS), joined(X, LAYERS), joined(RATE, 1))
    rim = (outer(V, LAYERS), outer(X, LAYERS), outer(RATE, 1))
    here, slope = state(*halo)
    rim_here, _ = state(*rim)
    in_edge, _ = edge_state(inside(*halo))
    rim_in_edge, _ = edge_state(inside(*rim))

    def triples(states, ends):
        found = [beside(a, e) for a, e in zip(states, ends)]
        return [tuple(f[i] for f in found) for i in range(3)]

    def edge_triples(past, at, within):
        left = tuple(jnp.where(even, a, b) for a, b in zip(past, within))
        right = tuple(jnp.where(even, b, a) for a, b in zip(past, within))
        return [left, at, right]

    def halves_of(slots):
        found = []
        for d in range(len(OFFSETS)):
            tally = (slots[0] == d).astype(F32)
            for other in slots[1:]:
                tally = tally + (other == d).astype(F32)
            found.append(0.5 * tally)
        return found

    def coupling(halves, centre, around, beyond, keep):
        eta, v = centre[:2]
        axis = eta.ndim - 2
        side = pull = part = 0.0
        for dx in (-1, 0, 1):
            eta_here, v_here = turn(eta, dx, axis), turn(v, dx, axis)
            sums = [0.0, 0.0, 0.0]
            for d, (ox, oy) in enumerate(OFFSETS):
                if ox != dx:
                    continue
                weight = turn(halves[d], dx, 0)
                if dx != 0:
                    weight = jnp.where(row == (3 if dx < 0 else 0), 0.0, weight)
                eta_n, v_n, x_n, deta_n = around[oy + 1]
                couple = weight * (eta_here + eta_n)
                drop = weight * (v_here - v_n)
                if keep:
                    cs[d] = couple
                    ds_[d] = drop
                sums = [sums[0] + couple, sums[1] + drop, sums[2] + (drop * deta_n - couple * x_n)]
            side, pull, part = (
                old + turn(new, -dx, axis) for old, new in zip((side, pull, part), sums)
            )
        for oy in (-1, 0, 1):
            weight = jnp.where(row == 0, halves[OFFSETS.index((-1, oy))], 0.0)
            weight = jnp.where(row == 3, halves[OFFSETS.index((1, oy))], weight)
            eta_n, v_n, x_n, deta_n = beyond[oy + 1]
            couple = weight * (eta + eta_n)
            drop = weight * (v - v_n)
            side, pull = side + couple, pull + drop
            part = part + (drop * deta_n - couple * x_n)
        return side, pull, part

    eta, v, x, deta = here
    links_here = jnp.where(core, own[SLOT : SLOT + 4], near[SLOT : SLOT + 4])
    rub = jnp.where(core, own[RUB], near[RUB])
    side, pull, part = coupling(
        halves_of([links_here[k] for k in range(4)]),
        here,
        triples(here, ends_at),
        triples(rim_here, rim_ends_at),
        True,
    )
    face = (0.5 * KZ) * (eta[:-1] + eta[1:])
    jump = (0.5 * KZ) * (v[1:] - v[:-1])

    def column_terms(x, deta):
        flux = face * (x[1:] - x[:-1]) + jump * (deta[1:] + deta[:-1])
        return jnp.concatenate([rub * x[:1] - flux[:1], flux[:-1] - flux[1:], flux[-1:]])

    image = side * x + pull * deta + part + column_terms(x, deta)
    img[...] = image
    resid = joined(LOAD, LAYERS) - image

    def of_edge(at):
        return jnp.where(even, edge0[:, at : at + 1], edge0[:, at - 1 : at])

    edge_side, edge_pull, edge_part = coupling(
        halves_of([of_edge(46 + 2 * k) for k in range(4)]),
        at_edge,
        edge_triples(past_edge, at_edge, in_edge),
        edge_triples(rim_past_edge, rim_at_edge, rim_in_edge),
        False,
    )
    eta_e, v_e, x_e, deta_e = at_edge
    edge_rub = of_edge(44)

    def upper_of(tile):
        return turn(tile, -2, 1)

    edge_face = jnp.where(top, 0.0, (0.5 * KZ) * (eta_e + upper_of(eta_e)))
    edge_jump = (0.5 * KZ) * (upper_of(v_e) - v_e)
    flux = edge_face * (upper_of(x_e) - x_e) + edge_jump * (upper_of(deta_e) + deta_e)
    flux = jnp.where(top, 0.0, flux)
    edge_image = edge_side * x_e + edge_pull * deta_e + edge_part - flux
    edge_image = edge_image + jnp.where(bottom, edge_rub * x_e, turn(flux, 2, 1))
    edge_resid = unpacked(edge_load - edge_image)

    side2 = [stacked(pair) for pair in zip(side, unpacked(edge_side))]
    face2 = [stacked(pair) for pair in zip(face, unpacked(edge_face))]
    ends_rub = jnp.where(lane < 64, edge0[:, 44:45], edge0[:, 43:44])
    middle = LAYERS // 2
    inverse2, inward2, outward2 = [None] * LAYERS, [None] * LAYERS, [None] * LAYERS

    def eliminate(layer, before, after):
        pivot = side2[layer]
        if layer == 0:
            pivot = pivot + stacked([rub, ends_rub])
        if after is not None:
            pivot = pivot + face2[after]
        if before is not None:
            previous = layer - 1 if layer < middle else layer + 1
            pivot = pivot + face2[before] - face2[before] * outward2[previous]
        inv = 1.0 / pivot
        inverse2[layer] = inv
        inward2[layer] = None if before is None else face2[before] * inv
        outward2[layer] = None if after is None else face2[after] * inv

    for step in range(middle):
        eliminate(step, step - 1 if step else None, step)
        layer = LAYERS - 1 - step
        eliminate(layer, layer if step else None, layer - 1)
    meet2 = 1.0 / (1.0 - outward2[middle - 1] * outward2[middle])

    def line_solve(rhs, inverse, inward, outward, meet):
        found = [None] * LAYERS
        for step in range(middle):
            for layer, previous in ((step, step - 1), (LAYERS - 1 - step, LAYERS - step)):
                found[layer] = rhs[layer] * inverse[layer]
                if step:
                    found[layer] = found[layer] + inward[layer] * found[previous]
        low, high = middle - 1, middle
        found[low] = (found[low] + outward[low] * found[high]) * meet
        found[high] = found[high] + outward[high] * found[low]
        for step in range(1, middle):
            for layer, previous in ((low - step, low - step + 1), (high + step, high + step - 1)):
                found[layer] = found[layer] + outward[layer] * found[previous]
        return found

    solved = line_solve(
        [stacked(p) for p in zip(resid, edge_resid)], inverse2, inward2, outward2, meet2
    )
    own_factors = [
        [a if a is None else a[0] for a in factor] for factor in (inverse2, inward2, outward2)
    ] + [meet2[0]]
    smooth = jnp.where(row_ok, stacked([a[0] for a in solved]), 0.0)
    ends = jnp.where(row_ok & half_ok, stacked([a[1] for a in solved]), 0.0)

    dsmooth = derived(slope, vertical(smooth))
    dends = derived(unpacked(edge_slope), vertical(ends))
    smooth_beside = beside(smooth, ends)
    dsmooth_beside = beside(dsmooth, dends)
    plain = resid - (side * smooth + pull * dsmooth)
    parts = []
    for dx in (-1, 0, 1):
        part = 0.0
        for d, (ox, oy) in enumerate(OFFSETS):
            if ox == dx:
                part = part + (cs[d] * smooth_beside[oy + 1] - ds_[d] * dsmooth_beside[oy + 1])
        parts.append(part)
    total = jnp.sum(plain, axis=0) - rub * smooth[0]
    for dx, part in zip((-1, 0, 1), parts):
        total = total + turn(jnp.sum(part, axis=0), -dx, 0)
    mean = jnp.where(core, total / LAYERS, 0.0)

    pieces, rest_of = [], mean
    for _ in range(2):
        large = rest_of * 65537.0
        piece = large - (large - rest_of)
        pieces.append(piece)
        rest_of = rest_of - piece
    pieces.append(rest_of)
    pieces = jnp.concatenate(pieces, axis=0)
    sums = lax.dot_general(
        jnp.concatenate([pieces, turn(pieces, -1, 0)], axis=1),
        jnp.concatenate(hot, axis=1),
        (((1,), (1,)), ((), ())),
        preferred_element_type=F32,
    )
    sums = sums[0:8] + sums[8:16] + sums[16:24]
    mine = jnp.where(lane[0:1] < AGG_DEV, sums[1:2], sums[5:6])
    rs[0] = mine
    place = lax.rem(py, 2) * n_hi + lax.div(py, 2)

    def push(group, dx, k):
        pltpu.make_async_remote_copy(
            src_ref=rs,
            dst_ref=rr.at[pl.ds(group * n_py + place, 1)],
            send_sem=gather_sem.at[group],
            recv_sem=gather_sem.at[3 + group],
            device_id=peer(dx, k),
            device_id_type=MESH,
        ).start()

    pl.semaphore_wait(complete, lines)
    for reach in range(n_py // 2, -1, -1):
        far_off = sorted({reach, (n_py - reach) % n_py})
        for group in (2, 1):
            dx, ok = pairs[group - 1]

            def push_all(group=group, dx=dx, far_off=far_off):
                for k in far_off:
                    push(group, dx, k)

            pl.when(ok)(push_all)
        for k in far_off:
            if k:
                push(0, 0, k)
    kept = pltpu.make_async_copy(rs, rr.at[pl.ds(place, 1)], gather_sem.at[3])
    kept.start()

    def gathered(sem, first, size):
        some = rr.at[pl.ds(first, size)]
        pltpu.make_async_copy(some, some, gather_sem.at[sem]).wait()

    after = plain - column_terms(smooth, dsmooth)
    for dx, part in zip((-1, 0, 1), parts):
        after = after + turn(part, -dx, 1)
    rest = line_solve([after[layer] for layer in range(LAYERS)], *own_factors)
    for layer in range(LAYERS):
        ans[layer] = smooth[layer] + rest[layer]
    for d, (dx, _) in enumerate(OFFSETS):
        ws[:, d] = turn(cs[d], -dx, 1)
    for layer, held in enumerate(line_solve([ws[i] for i in range(LAYERS)], *own_factors)):
        ws[layer] = held

    received(coarse)
    operators = []
    for f, c in ((cf, cc), (cf_near.at[0], cc_near.at[0]), (cf_near.at[1], cc_near.at[1])):
        scale = OMEGA / f[0]
        cols = [c[k] for k in range(4)]
        weights = [f[1 + k] * scale for k in range(4)]
        bits = [
            [((a >> (7 + b)) & 1) == 1 for b in range((n_hi - 1).bit_length())] for a in cols
        ]
        operators.append((scale, weights, bits, [a & 127 for a in cols]))
    agg_all = jnp.where(core, own[AGG], near[AGG])
    agg_all = jnp.where(row_ok, agg_all, 0.0).astype(I32)
    sent(round1 + coarse)
    gathered(0, 0, n_py - 1)
    for group, (_, ok) in enumerate(pairs):
        pl.when(ok)(functools.partial(gathered, 1 + group, 0, n_py))
    low = lax.broadcasted_iota(I32, (n_hi, 128), 1) < AGG_DEV

    def picked(source, at):
        return jnp.take_along_axis(source, at, axis=1, mode="promise_in_bounds")

    for g, (scale, weights, col_bits, col_lo) in enumerate(operators):
        if g == 0:
            gathered(3, 0, n_py)
        else:
            pl.when(pairs[g - 1][1])(functools.partial(gathered, 3 + g, g * n_py, n_py))
        evens = rr[g * n_py : g * n_py + n_hi, 0, :]
        odds = rr[g * n_py + n_hi : (g + 1) * n_py, 0, :]
        target = [
            jnp.where(low, evens, turn(odds, AGG_DEV, 1)) * scale,
            jnp.where(low, turn(evens, AGG_DEV, 1), odds) * scale,
        ]
        iterate = target
        for _ in range(CITERS - 1):
            later = []
            for c in range(2):
                rows = [
                    jnp.broadcast_to(iterate[c][h : h + 1], (n_hi, 128)) for h in range(n_hi)
                ]
                value = (1.0 - OMEGA) * iterate[c] + target[c]
                for k in range(4):
                    found = [picked(r, col_lo[k]) for r in rows]
                    for bit in col_bits[k]:
                        found = [
                            jnp.where(bit, b, a) for a, b in zip(found[::2], found[1::2])
                        ]
                    value = value - weights[k] * found[0]
                later.append(value)
            iterate = later
        xs[g, 0] = iterate[0]
        xs[g, 1] = iterate[1]

    def corrected(owner, at):
        h = pl.ds(lax.div(owner, 2), 1)
        below, here, above = (
            jnp.where(sub < 4, xs[g, 0, h, :], xs[g, 1, h, :]) for g in (2 - odd, 0, 1 + odd)
        )
        source = jnp.where(row == 0, below, jnp.where(row == 3, above, here))
        return picked(source, at + AGG_DEV * lax.rem(owner, 2))

    edge_agg = edge0.astype(I32)
    agg_left = jnp.broadcast_to(edge_agg[:, 42:43], (8, 128))
    agg_right = jnp.broadcast_to(edge_agg[:, 41:42], (8, 128))
    corr = jnp.where(row_ok, corrected(py, agg_all), 0.0)
    corr_edge = jnp.where(
        half == 0,
        corrected(wrap(py - 1, n_py), agg_left),
        corrected(wrap(py + 1, n_py), agg_right),
    )
    corr_edge = jnp.where(row_ok & half_ok, corr_edge, 0.0)
    corr_beside = beside(corr, corr_edge)
    result = ans[...]
    for d, (dx, dy) in enumerate(OFFSETS):
        result = result + ws[:, d] * turn(corr_beside[dy + 1], -dx, 0)
    ans[...] = result


def write_out(image, answer, image_out, answer_out, sems):
    copies = []
    for c in range(2):
        rows = pl.ds(4 * c + 1, 2)
        copies.append(pltpu.make_async_copy(image.at[:, rows], image_out.at[c], sems.at[c]))
        copies.append(pltpu.make_async_copy(answer.at[:, rows], answer_out.at[c], sems.at[2 + c]))
    for copy in copies:
        copy.start()
    for copy in copies:
        copy.wait()


def solution(mesh):
    n_px, n_py = mesh.shape["px"], mesh.shape["py"]
    n_hi = n_py // 2
    n_sends = 18

    def body(
        velocity, direction, forcing, softness, friction, links, aggregate, diag, vals, cols
    ):
        block = jax.ShapeDtypeStruct(velocity.shape, F32)
        wide = jax.ShapeDtypeStruct((LAYERS, 8, 128), F32)
        results = pl.pallas_call(
            functools.partial(kernel, n_px, n_py),
            out_shape=(wide, wide),
            in_specs=[pl.BlockSpec(memory_space=pltpu.HBM)] * 10,
            out_specs=[pl.BlockSpec(memory_space=pltpu.VMEM)] * 2,
            scratch_shapes=[
                pltpu.VMEM((PLANES, 8, 128), F32),
                pltpu.VMEM((PLANES, 8, 128), F32),
                pltpu.VMEM((FAR, 8, 128), F32),
                pltpu.VMEM((4, 8, 128), I32),
                pltpu.VMEM((8, 128), I32),
                pltpu.VMEM((5, n_hi, 128), F32),
                pltpu.VMEM((4, n_hi, 128), I32),
                pltpu.VMEM((2, 5, n_hi, 128), F32),
                pltpu.VMEM((2, 4, n_hi, 128), I32),
                pltpu.VMEM((3, 8, 128), F32),
                pltpu.VMEM((6, 3, 8, 128), F32),
                pltpu.VMEM((1, 1, 128), F32),
                pltpu.VMEM((3 * n_py, 1, 128), F32),
                pltpu.VMEM((3, 2, n_hi, 128), F32),
                pltpu.VMEM((8, LAYERS, 8, 128), F32),
                pltpu.VMEM((8, LAYERS, 8, 128), F32),
                pltpu.VMEM((LAYERS, 8, 8, 128), F32),
                pltpu.SemaphoreType.DMA((23,)),
                pltpu.SemaphoreType.DMA((n_sends,)),
                pltpu.SemaphoreType.DMA((n_sends,)),
                pltpu.SemaphoreType.DMA((6,)),
                pltpu.SemaphoreType.REGULAR,
                pltpu.SemaphoreType.REGULAR,
            ],
            compiler_params=pltpu.CompilerParams(
                collective_id=0, has_side_effects=True, vmem_limit_bytes=32 * 1024 * 1024
            ),
        )(
            *(
                pltpu.with_memory_space_constraint(a, pltpu.HBM)
                for a in (
                    velocity,
                    direction,
                    forcing,
                    softness,
                    friction,
                    links,
                    aggregate,
                    diag.reshape(n_hi, 128),
                    vals.reshape(4, n_hi, 128).transpose(1, 0, 2),
                    cols.reshape(4, n_hi, 128).transpose(1, 0, 2),
                )
            )
        )
        return pl.pallas_call(
            write_out,
            out_shape=(block, block),
            in_specs=[pl.BlockSpec(memory_space=pl.ANY)] * 2,
            out_specs=[pl.BlockSpec(memory_space=pltpu.HBM)] * 2,
            scratch_shapes=[pltpu.SemaphoreType.DMA((4,))],
            compiler_params=pltpu.CompilerParams(vmem_limit_bytes=8 * 1024 * 1024),
        )(*results)

    return jax.shard_map(
        body,
        mesh=mesh,
        in_specs=(
            P(None, None, "px", "py"),
            P(None, None, "px", "py"),
            P(None, None, "px", "py"),
            P("px", "py"),
            P("px", "py"),
            P(None, "px", "py"),
            P("px", "py"),
            P("px"),
            P(None, "px"),
            P(None, "px"),
        ),
        out_specs=(P(None, None, "px", "py"), P(None, None, "px", "py")),
        check_vma=False,
    )
```
